32 devices in a mesh: rep: 2 (over y), ch: 4 (over z), row: 2 (over x), sub: 2 (over core).
Axes of the slice: x: 2, y: 2, z: 4, core: 2. Of those that a mesh axis runs over, the one named last changes fastest.
Arguments:
- pair: bfloat16 [1024, 512, 128], P(('rep', 'row', 'sub'), 'ch'), parts along dimension 0, may hold values from -6 to 6
- grad_out: bfloat16 [1024, 512, 128], P(('rep', 'row', 'sub'), 'ch'), parts along dimension 0, may hold values from -6 to 6
- token_mask: int32 [1024], P('rep'), parts along dimension 0, may hold values 0 or 1
- ln_gain: float32 [128], replicated, may hold values from 0.1 to 1.9
- proj_weights: bfloat16 [4, 128, 128], replicated, may hold values from -0.5 to 0.5
- gate_weight: bfloat16 [128, 128], replicated, may hold values from -0.5 to 0.5
- out_weight: bfloat16 [128, 128], replicated, may hold values from -0.5 to 0.5
- out_gain: float32 [128], replicated, may hold values from 0.1 to 1.9
Outputs:
- grad_pair: bfloat16 [1024, 512, 128], P(('rep', 'row', 'sub'), 'ch'), parts along dimension 0
The draws below stay inside these ranges and needn't reach their ends.
There are 2 independent parts, one for each index of `rep`. The reference program is written for one: setup_inputs(seed, part) draws one part's arguments, and reference() takes and returns one part's arrays. A program takes and returns all parts, laid end to end along the dimension named above; an argument that names none is the same for every part. Nothing has to cross between parts.
All inputs are finite; a program needn't handle non-finite values.
Results may differ from the reference program's by a relative error of at most 0.0095.
Values may be sent and summed in bfloat16 or wider, within the bound.
No kernel may reach another device: no remote copies, remote signals or barrier semaphores. Data moves between devices by JAX's collectives and lax.ppermute only.
A program may use at most 256 MiB of HBM per device.

```python
import jax
import jax.numpy as jnp
from jax import lax

C = 128
N = 512
ROWS_BLOCK = 128


def plant(array, key, smallest, largest):
    spot = [jax.random.randint(jax.random.fold_in(key, axis), (), 0, length) for axis, length in enumerate(array.shape)]
    longest = array.shape.index(max(array.shape))
    neighbour = spot[:longest] + [(spot[longest] + 1) % array.shape[longest]] + spot[longest + 1:]
    return array.at[tuple(spot)].set(smallest).at[tuple(neighbour)].set(largest)


def shard_levels(stream_key, shape, split, least, high):
    gain, own = 1.0, jax.random.fold_in(stream_key, 6)
    for position, blocks in split:
        heights = jnp.exp(jax.random.uniform(jax.random.fold_in(own, position), (blocks,), jnp.float32, least / len(split), high / len(split)))
        gain = gain * jnp.repeat(heights, shape[position] // blocks).reshape([-1 if axis == position else 1 for axis in range(len(shape))])
    return gain


def bell_draw(rng, shape, spread, most, cuts=(), kind=jnp.bfloat16):
    entries = jax.random.normal(rng, shape, jnp.float32) * spread
    if len(cuts) > 0:
        entries = shard_levels(rng, shape, cuts, -0.22, 0.18) * entries
    return jnp.clip(entries, min=-most, max=most).astype(kind)


def setup_inputs(seed: int = 0, part: int = 0) -> dict:
    key_list = jax.random.split(jax.random.key(seed), 9)
    part_splits = jax.random.split(jax.random.fold_in(key_list[8], part), 9)
    pair = bell_draw(part_splits[0], (N, N, C), 1.0, 6.0, ((0, 4), (1, 4)))
    grad_out = bell_draw(part_splits[1], (N, N, C), 1.0, 6.0, ((0, 4), (1, 4)))
    token_mask = plant((jax.random.randint(part_splits[2], (N,), 0, 8) < 7).astype(jnp.int32), jax.random.fold_in(part_splits[2], 1), 0, 1)
    ln_gain = jnp.clip(1.0 + 0.18 * jax.random.normal(key_list[3], (C,), jnp.float32), 0.1, 1.9)
    proj_weights = bell_draw(key_list[4], (4, C, C), C ** -0.5, 0.5)
    gate_weight = bell_draw(key_list[5], (C, C), C ** -0.5, 0.5)
    out_weight = bell_draw(key_list[6], (C, C), C ** -0.5, 0.5)
    out_gain = jnp.clip(1.0 + 0.18 * jax.random.normal(key_list[7], (C,), jnp.float32), 0.1, 1.9)
    return dict(pair=pair, grad_out=grad_out, token_mask=token_mask, ln_gain=ln_gain, proj_weights=proj_weights, gate_weight=gate_weight, out_weight=out_weight, out_gain=out_gain)


epsilon = 1e-05

def norm_parts(values):
    center = values - lax.optimization_barrier(jnp.mean(values, axis=-1, keepdims=True))
    scaled = lax.rsqrt(lax.optimization_barrier(jnp.mean(center * center, axis=-1, keepdims=True)) + epsilon)
    return (center * scaled, scaled)

def norm_back(grad_hat, normal, scaled):
    return scaled * (grad_hat - lax.optimization_barrier(jnp.mean(grad_hat, axis=-1, keepdims=True)) - normal * lax.optimization_barrier(jnp.mean(grad_hat * normal, axis=-1, keepdims=True)))

def project(values, weight):
    return jnp.einsum('ijd,dc->ijc', values.astype(jnp.float32), weight.astype(jnp.float32))

def project_back(values, weight):
    return jnp.einsum('ijc,dc->ijd', values.astype(jnp.float32), weight.astype(jnp.float32))

def reference(pair, grad_out, token_mask, ln_gain, proj_weights, gate_weight, out_weight, out_gain):
    pair_hat, pair_scale = norm_parts(pair.astype(jnp.float32))
    normed = (pair_hat * ln_gain).astype(jnp.bfloat16)
    mask_float = token_mask.astype(jnp.float32)
    pair_mask = (mask_float[:, None] * mask_float[None, :])[:, :, None]
    left_value = project(normed, proj_weights[0])
    left_gate = jax.nn.sigmoid(project(normed, proj_weights[1]))
    right_value = project(normed, proj_weights[2])
    right_gate = jax.nn.sigmoid(project(normed, proj_weights[3]))
    left = (pair_mask * left_gate * left_value).astype(jnp.bfloat16)
    right = (pair_mask * right_gate * right_value).astype(jnp.bfloat16)
    combined = jnp.einsum('ikc,jkc->ijc', left.astype(jnp.float32), right.astype(jnp.float32)).astype(jnp.bfloat16)
    comb_hat, comb_scale = norm_parts(combined.astype(jnp.float32))
    comb_normed = (comb_hat * out_gain).astype(jnp.bfloat16)
    out_linear = project(comb_normed, out_weight)
    gate_value = jax.nn.sigmoid(project(normed, gate_weight))
    grad_gate = grad_out.astype(jnp.float32) * out_linear
    grad_linear = (grad_out.astype(jnp.float32) * gate_value).astype(jnp.bfloat16)
    grad_normal = project_back(grad_linear, out_weight)
    grad_comb = norm_back(grad_normal * out_gain, comb_hat, comb_scale).astype(jnp.bfloat16)
    grad_left = jnp.einsum('ijc,jkc->ikc', grad_comb.astype(jnp.float32), right.astype(jnp.float32)).astype(jnp.bfloat16)
    total = jnp.zeros(pair.shape, jnp.float32)
    for block in range(N // ROWS_BLOCK):
        low = block * ROWS_BLOCK
        grad_block = grad_comb[low:low + ROWS_BLOCK].astype(jnp.float32)
        left_block = left[low:low + ROWS_BLOCK].astype(jnp.float32)
        partial_sum = jnp.einsum('ijc,ikc->jkc', grad_block, left_block)
        rounded = lax.optimization_barrier(partial_sum.astype(jnp.bfloat16))
        total = total + rounded.astype(jnp.float32)
    grad_right = total.astype(jnp.bfloat16)
    left_masked = grad_left.astype(jnp.float32) * pair_mask
    right_masked = grad_right.astype(jnp.float32) * pair_mask
    terms = [(left_masked * left_gate).astype(jnp.bfloat16), (left_masked * left_value * left_gate * (1.0 - left_gate)).astype(jnp.bfloat16), (right_masked * right_gate).astype(jnp.bfloat16), (right_masked * right_value * right_gate * (1.0 - right_gate)).astype(jnp.bfloat16)]
    grad_sigm = (grad_gate * gate_value * (1.0 - gate_value)).astype(jnp.bfloat16)
    grad_normed = project_back(grad_sigm, gate_weight)
    for index in range(4):
        grad_normed = grad_normed + project_back(terms[index], proj_weights[index])
    return norm_back(grad_normed * ln_gain, pair_hat, pair_scale).astype(jnp.bfloat16)
```

```python
import functools

import jax
import jax.numpy as jnp
from jax import lax
from jax.experimental import pallas as pl
from jax.experimental.pallas import tpu as pltpu
from jax.sharding import PartitionSpec as P

epsilon = 1e-05
F32 = jnp.float32
BF16 = jnp.bfloat16
VMEM_LIMIT = 48 * 1024 * 1024


def dot(a, b, ca, cb):
    return lax.dot_general(a, b, (((ca,), (cb,)), ((), ())), preferred_element_type=F32)


def norm_rows(pair_block, gain):
    x = pair_block.astype(F32)
    center = x - jnp.mean(x, axis=1, keepdims=True)
    scaled = lax.rsqrt(jnp.mean(center * center, axis=1, keepdims=True) + epsilon)
    hat = center * scaled
    return hat, scaled, (hat * gain).astype(BF16)


def rows_of(ref, first, count):
    block = ref[first:first + count]
    return block.reshape(count * block.shape[1], block.shape[2])


def load_chan(ref, first, count):
    parts = [ref[:, first + t] for t in range(count)]
    parts = [p.astype(F32).reshape(p.shape[0] * p.shape[1], p.shape[2]) for p in parts]
    return parts[0] if count == 1 else jnp.concatenate(parts, axis=1)


def store_chan(ref, first, count, value):
    groups, _, chans, cols = ref.shape
    for t in range(count):
        part = value[:, t * cols:(t + 1) * cols] if count > 1 else value
        ref[:, first + t] = part.reshape(groups, chans, cols).astype(BF16)


def project_kernel(step, pair_ref, mask_ref, gain_ref, weight_ref, out_ref):
    rows, cols, chans = pair_ref.shape
    for first in range(0, rows, step):
        _, _, normed = norm_rows(rows_of(pair_ref, first, step), gain_ref[...])
        both = dot(weight_ref[...], normed, 1, 1)
        mask = mask_ref[0, :, first * cols:(first + step) * cols]
        store_chan(out_ref, first, step, mask * jax.nn.sigmoid(both[chans:]) * both[:chans])


def middle_kernel(
    step, pair_ref, gout_ref, comb_ref, gain_ref, gate_t_ref, out_w_ref, out_t_ref, out_gain_ref, eye_ref,
    gcomb_ref, sigm_ref,
):
    rows, cols, chans = pair_ref.shape
    out_gain = out_gain_ref[...]
    for first in range(0, rows, step):
        _, _, normed = norm_rows(rows_of(pair_ref, first, step), gain_ref[...])
        gate = jax.nn.sigmoid(dot(gate_t_ref[...], normed, 1, 1))
        gout = dot(eye_ref[...], rows_of(gout_ref, first, step), 1, 1)
        comb = load_chan(comb_ref, first, step)
        center = comb - jnp.mean(comb, axis=0, keepdims=True)
        scaled = lax.rsqrt(jnp.mean(center * center, axis=0, keepdims=True) + epsilon)
        hat = center * scaled
        lin = dot(out_t_ref[...], (hat * out_gain).astype(BF16), 1, 0)
        grad_lin = (gout * gate).astype(BF16)
        h = dot(out_w_ref[...], grad_lin, 1, 0) * out_gain
        grad = scaled * (
            h - jnp.mean(h, axis=0, keepdims=True) - hat * jnp.mean(h * hat, axis=0, keepdims=True)
        )
        store_chan(gcomb_ref, first, step, grad)
        sigm = (gout * lin * gate * (1.0 - gate)).astype(BF16)
        for t in range(step):
            sigm_ref[first + t] = sigm[:, t * cols:(t + 1) * cols] if step > 1 else sigm


def last_kernel(
    step, pair_ref, left_ref, right_ref, sigm_ref, mask_ref, gain_ref, weight_ref, held_ref, out_ref
):
    del held_ref
    rows, cols, chans = pair_ref.shape
    gain = gain_ref[...]
    weight = weight_ref[...]
    for first in range(0, rows, step):
        hat, scaled, normed = norm_rows(rows_of(pair_ref, first, step), gain)
        mask = mask_ref[0, :, first * cols:(first + step) * cols]
        proj = dot(weight[:4 * chans], normed, 1, 1)
        terms = []
        for which, ref in enumerate((left_ref, right_ref)):
            grad = load_chan(ref, first, step) * mask
            value = proj[2 * which * chans:(2 * which + 1) * chans]
            gate = jax.nn.sigmoid(proj[(2 * which + 1) * chans:(2 * which + 2) * chans])
            through = grad * gate
            terms += [through.astype(BF16), (through * value * (1.0 - gate)).astype(BF16)]
        parts = [sigm_ref[first + t] for t in range(step)]
        terms.append(parts[0] if step == 1 else jnp.concatenate(parts, axis=1))
        g = dot(jnp.concatenate(terms, axis=0), weight, 0, 0) * gain
        grad_in = scaled * (
            g - jnp.mean(g, axis=1, keepdims=True) - hat * jnp.mean(g * hat, axis=1, keepdims=True)
        )
        out_ref[first:first + step] = grad_in.reshape(step, cols, chans).astype(BF16)


def local(group, chunks, pair, grad_out, token_mask, ln_gain, proj_weights, gate_weight, out_weight, out_gain):
    rows, cols, chans = pair.shape
    peers = lax.axis_size(group)
    row_blocks = lax.axis_size(group[1:])
    col_blocks = peers // row_blocks
    own = chans // peers
    tokens = rows * row_blocks
    part_rows = rows // chunks
    block = min(8, part_rows)
    blocks = part_rows // block
    step = 4 if cols % 128 == 0 and block % 4 == 0 else 1

    mask_float = token_mask.astype(F32)
    row_mask = lax.dynamic_slice_in_dim(mask_float, lax.axis_index(group[1:]) * rows, rows)
    col_mask = lax.dynamic_slice_in_dim(mask_float, lax.axis_index(group[0]) * cols, cols)
    mask = (row_mask[:, None] * col_mask[None, :]).reshape(rows // block, 1, block * cols)
    gain = ln_gain.reshape(1, chans)
    proj_t = jnp.swapaxes(proj_weights, 1, 2)
    left_w = proj_t[:2].reshape(2 * chans, chans)
    right_w = proj_t[2:].reshape(2 * chans, chans)
    gate_t = gate_weight.T
    all_w = jnp.concatenate([left_w, right_w, gate_t], axis=0)
    eye = jnp.eye(chans, dtype=BF16)

    params = pltpu.CompilerParams(vmem_limit_bytes=VMEM_LIMIT)

    def cost(flops_per_pair, arrays, pairs):
        return pl.CostEstimate(
            flops=flops_per_pair * pairs, bytes_accessed=arrays * pairs * chans * 2, transcendentals=chans * pairs
        )

    def row_spec(first):
        return pl.BlockSpec((block, cols, chans), lambda s: (first + s, 0, 0))

    def mask_spec(first):
        return pl.BlockSpec((1, 1, block * cols), lambda s: (first + s, 0, 0))

    def whole(array):
        return pl.BlockSpec(array.shape, lambda s: (0,) * array.ndim)

    chan_spec = pl.BlockSpec((peers, block, own, cols), lambda s: (0, s, 0, 0))
    sigm_spec = pl.BlockSpec((block, chans, cols), lambda s: (s, 0, 0))

    def project(weight, first, count):
        return pl.pallas_call(
            functools.partial(project_kernel, step),
            grid=(count,),
            in_specs=[row_spec(first), mask_spec(first), whole(gain), whole(weight)],
            out_specs=chan_spec,
            out_shape=jax.ShapeDtypeStruct((peers, count * block, own, cols), BF16),
            compiler_params=params,
            cost_estimate=cost(4 * chans * chans, 2, count * block * cols),
        )(pair, mask, gain, weight)

    def exchange(array):
        return lax.all_to_all(array, group, split_axis=0, concat_axis=0, tiled=True)

    def by_channel(array):
        count = array.shape[1]
        array = array.reshape(col_blocks, row_blocks, count, own, cols)
        return jnp.transpose(array, (3, 1, 2, 0, 4)).reshape(own, row_blocks * count, tokens)

    def by_owner(array):
        count = array.shape[1] // row_blocks
        array = array.astype(BF16).reshape(own, row_blocks, count, col_blocks, cols)
        return jnp.transpose(array, (3, 1, 2, 0, 4)).reshape(peers, count, own, cols)

    def batch_dot(a, b, ca, cb):
        return lax.dot_general(a, b, (((ca,), (cb,)), ((0,), (0,))), preferred_element_type=F32)

    def middle(comb, first):
        out_t = out_weight.T
        gain_col = out_gain.reshape(chans, 1)
        return pl.pallas_call(
            functools.partial(middle_kernel, step),
            grid=(blocks,),
            in_specs=[row_spec(first), row_spec(first), chan_spec, whole(gain), whole(gate_t), whole(out_weight),
                      whole(out_t), whole(gain_col), whole(eye)],
            out_specs=[chan_spec, sigm_spec],
            out_shape=[
                jax.ShapeDtypeStruct((peers, part_rows, own, cols), BF16),
                jax.ShapeDtypeStruct((part_rows, chans, cols), BF16),
            ],
            compiler_params=params,
            cost_estimate=cost(8 * chans * chans, 5, part_rows * cols),
        )(pair, grad_out, comb, gain, gate_t, out_weight, out_t, gain_col, eye)

    def last(left_grad, right_grad, sigm, first, held):
        return pl.pallas_call(
            functools.partial(last_kernel, step),
            grid=(blocks,),
            in_specs=[row_spec(first), chan_spec, chan_spec, sigm_spec, mask_spec(first), whole(gain), whole(all_w),
                      pl.BlockSpec(memory_space=pl.ANY)],
            out_specs=row_spec(first),
            out_shape=jax.ShapeDtypeStruct((rows, cols, chans), BF16),
            input_output_aliases={7: 0},
            compiler_params=params,
            cost_estimate=cost(18 * chans * chans, 5, part_rows * cols),
        )(pair, left_grad, right_grad, sigm, mask, gain, all_w, held)

    right = by_channel(exchange(project(right_w, 0, rows // block)))
    firsts = [part * blocks for part in range(chunks)]
    lefts = [by_channel(exchange(project(left_w, first, blocks))) for first in firsts]
    sigms, left_grads, grad_parts = [], [], []
    for first, left in zip(firsts, lefts):
        comb = exchange(by_owner(batch_dot(left, right, 2, 2)))
        grad_comb, sigm = middle(comb, first)
        sigms.append(sigm)
        grad_comb = by_channel(exchange(grad_comb))
        left_grads.append(exchange(by_owner(batch_dot(grad_comb, right, 2, 1))))
        grad_parts.append(batch_dot(grad_comb, left, 1, 1))
    grad_right = by_owner(functools.reduce(jnp.add, grad_parts))
    right_grads = [exchange(grad_right[:, p * part_rows:(p + 1) * part_rows]) for p in range(chunks)]
    out = jnp.zeros((rows, cols, chans), BF16)
    for first, left_grad, right_grad, sigm in zip(firsts, left_grads, right_grads, sigms):
        out = last(left_grad, right_grad, sigm, first, out)
    return out


def solution(mesh):
    spread = P(("rep", "row", "sub"), "ch", None)
    return jax.shard_map(
        functools.partial(local, ("ch", "row", "sub"), 2),
        mesh=mesh,
        in_specs=(spread, spread, P("rep"), P(), P(), P(), P(), P()),
        out_specs=spread,
        check_vma=False,
    )
```

```python
import functools

import jax
import jax.numpy as jnp
from jax import lax
from jax.experimental import pallas as pl
from jax.experimental.pallas import tpu as pltpu
from jax.sharding import Mesh
from jax.sharding import PartitionSpec as P

epsilon = 1e-05
F32 = jnp.float32
BF16 = jnp.bfloat16
VMEM_LIMIT = 48 * 1024 * 1024
GROUP = ("rep", "low", "row", "sub")
SWAP = ("rep", "high")


def dot(a, b, ca, cb):
    return lax.dot_general(a, b, (((ca,), (cb,)), ((), ())), preferred_element_type=F32)


def norm_rows(pair_block, gain):
    x = pair_block.astype(F32)
    center = x - jnp.mean(x, axis=1, keepdims=True)
    scaled = lax.rsqrt(jnp.mean(center * center, axis=1, keepdims=True) + epsilon)
    hat = center * scaled
    return hat, scaled, (hat * gain).astype(BF16)


def rows_of(ref, first, count):
    block = ref[first:first + count]
    return block.reshape(count * block.shape[1], block.shape[2])


def load_chan(ref, slot, first, count):
    parts = [ref[:, slot, first + t] for t in range(count)]
    parts = [p.astype(F32).reshape(p.shape[0] * p.shape[1], p.shape[2]) for p in parts]
    return parts[0] if count == 1 else jnp.concatenate(parts, axis=1)


def store_chan(ref, slot, first, count, value):
    groups, _, _, chans, cols = ref.shape
    for t in range(count):
        part = value[:, t * cols:(t + 1) * cols] if count > 1 else value
        ref[:, slot, first + t] = part.reshape(groups, chans, cols).astype(BF16)


def project_kernel(step, flip_ref, pair_a, pair_b, mask_a, mask_b, gain_ref, weight_ref, left_ref, right_ref):
    rows, cols, chans = pair_a.shape
    for which, (pair_ref, mask_ref) in enumerate(((pair_a, mask_a), (pair_b, mask_b))):
        slot = flip_ref[which]
        for first in range(0, rows, step):
            _, _, normed = norm_rows(rows_of(pair_ref, first, step), gain_ref[...])
            proj = dot(weight_ref[...], normed, 1, 1)
            mask = mask_ref[0, :, first * cols:(first + step) * cols]
            left = mask * jax.nn.sigmoid(proj[chans:2 * chans]) * proj[:chans]
            right = mask * jax.nn.sigmoid(proj[3 * chans:]) * proj[2 * chans:3 * chans]
            store_chan(left_ref, slot, first, step, left)
            store_chan(right_ref, slot, first, step, right)


def middle_kernel(
    step, flip_ref, pair_a, pair_b, gout_a, gout_b, comb_ref, gain_ref, gate_t_ref, out_w_ref, out_t_ref,
    out_gain_ref, eye_ref, gcomb_ref, sigm_ref,
):
    rows, cols, chans = pair_a.shape
    out_gain = out_gain_ref[...]
    for which, (pair_ref, gout_ref) in enumerate(((pair_a, gout_a), (pair_b, gout_b))):
        slot = flip_ref[which]
        for first in range(0, rows, step):
            _, _, normed = norm_rows(rows_of(pair_ref, first, step), gain_ref[...])
            gate = jax.nn.sigmoid(dot(gate_t_ref[...], normed, 1, 1))
            gout = dot(eye_ref[...], rows_of(gout_ref, first, step), 1, 1)
            comb = load_chan(comb_ref, slot, first, step)
            center = comb - jnp.mean(comb, axis=0, keepdims=True)
            scaled = lax.rsqrt(jnp.mean(center * center, axis=0, keepdims=True) + epsilon)
            hat = center * scaled
            lin = dot(out_t_ref[...], (hat * out_gain).astype(BF16), 1, 0)
            grad_lin = (gout * gate).astype(BF16)
            h = dot(out_w_ref[...], grad_lin, 1, 0) * out_gain
            grad = scaled * (
                h - jnp.mean(h, axis=0, keepdims=True) - hat * jnp.mean(h * hat, axis=0, keepdims=True)
            )
            store_chan(gcomb_ref, slot, first, step, grad)
            sigm = (gout * lin * gate * (1.0 - gate)).astype(BF16)
            for t in range(step):
                sigm_ref[which, first + t] = sigm[:, t * cols:(t + 1) * cols] if step > 1 else sigm


def last_kernel(
    step, flip_ref, pair_a, pair_b, left_ref, right_ref, sigm_ref, mask_a, mask_b, gain_ref, weight_ref, out_a, out_b
):
    rows, cols, chans = pair_a.shape
    gain = gain_ref[...]
    weight = weight_ref[...]
    for which, (pair_ref, mask_ref, out_ref) in enumerate(((pair_a, mask_a, out_a), (pair_b, mask_b, out_b))):
        slot = flip_ref[which]
        for first in range(0, rows, step):
            hat, scaled, normed = norm_rows(rows_of(pair_ref, first, step), gain)
            mask = mask_ref[0, :, first * cols:(first + step) * cols]
            proj = dot(weight[:4 * chans], normed, 1, 1)
            terms = []
            for side, ref in enumerate((left_ref, right_ref)):
                grad = load_chan(ref, slot, first, step) * mask
                value = proj[2 * side * chans:(2 * side + 1) * chans]
                gate = jax.nn.sigmoid(proj[(2 * side + 1) * chans:(2 * side + 2) * chans])
                through = grad * gate
                terms += [through.astype(BF16), (through * value * (1.0 - gate)).astype(BF16)]
            parts = [sigm_ref[which, first + t] for t in range(step)]
            terms.append(parts[0] if step == 1 else jnp.concatenate(parts, axis=1))
            g = dot(jnp.concatenate(terms, axis=0), weight, 0, 0) * gain
            grad_in = scaled * (
                g - jnp.mean(g, axis=1, keepdims=True) - hat * jnp.mean(g * hat, axis=1, keepdims=True)
            )
            out_ref[first:first + step] = grad_in.reshape(step, cols, chans).astype(BF16)


def local(chunks, pair, grad_out, token_mask, ln_gain, proj_weights, gate_weight, out_weight, out_gain):
    full_rows, cols, chans = pair.shape
    halves = lax.axis_size("rep")
    low = lax.axis_size("low")
    row_blocks = lax.axis_size(("row", "sub"))
    peers = halves * low * row_blocks
    own = chans // peers
    tokens = full_rows * row_blocks
    half_rows = full_rows // halves
    rows = half_rows // chunks
    block = min(4, rows)
    blocks = rows // block
    step = 4 if cols % 128 == 0 and block % 4 == 0 else 1
    rep, high = lax.axis_index("rep"), lax.axis_index("high")

    places = [(y, b) for y in range(halves) for b in range(halves)]
    at = {place: n for n, place in enumerate(places)}
    goes = [
        [(at[y, b], at[b, y]) for y, b in places],
        [(at[y, b], at[1 - b, y]) for y, b in places],
    ]
    back = [[(d, s) for s, d in perm] for perm in goes]
    half_of = [high, 1 - high]

    def move_in(array, part):
        return [
            lax.ppermute(
                lax.dynamic_slice_in_dim(array, half_of[w] * half_rows + part * rows, rows), SWAP, goes[w]
            )
            for w in range(2)
        ]

    pairs = [move_in(pair, part) for part in range(chunks)]
    mask_float = lax.ppermute(token_mask.astype(F32), SWAP, goes[0])
    gouts = [move_in(grad_out, part) for part in range(chunks)]

    flip = jnp.stack([rep, 1 - rep]).astype(jnp.int32)
    row_mask = lax.dynamic_slice_in_dim(
        mask_float, lax.axis_index(("row", "sub")) * full_rows + rep * half_rows, half_rows
    )

    def pair_mask(slot):
        col_mask = lax.dynamic_slice_in_dim(mask_float, (slot * low + lax.axis_index("low")) * cols, cols)
        return (row_mask[:, None] * col_mask[None, :]).reshape(half_rows // block, 1, block * cols)

    masks = [pair_mask(rep), pair_mask(1 - rep)]
    gain = ln_gain.reshape(1, chans)
    gain_col = out_gain.reshape(chans, 1)
    proj_t = jnp.swapaxes(proj_weights, 1, 2).reshape(4 * chans, chans)
    gate_t = gate_weight.T
    out_t = out_weight.T
    all_w = jnp.concatenate([proj_t, gate_t], axis=0)
    eye = jnp.eye(chans, dtype=BF16)

    row_spec = pl.BlockSpec((block, cols, chans), lambda s, f: (s, 0, 0))
    chan_spec = pl.BlockSpec((peers, halves, block, own, cols), lambda s, f: (0, 0, s, 0, 0))
    sigm_spec = pl.BlockSpec((halves, block, chans, cols), lambda s, f: (0, s, 0, 0))
    row_shape = jax.ShapeDtypeStruct((rows, cols, chans), BF16)
    chan_shape = jax.ShapeDtypeStruct((peers, halves, rows, own, cols), BF16)
    sigm_shape = jax.ShapeDtypeStruct((halves, rows, chans, cols), BF16)

    def mask_spec(part):
        return pl.BlockSpec((1, 1, block * cols), lambda s, f: (part * blocks + s, 0, 0))

    def whole(array):
        return pl.BlockSpec(array.shape, lambda s, f: (0,) * array.ndim)

    def call(kernel, in_specs, out_specs, out_shape, flops, arrays, operands):
        count = halves * rows * cols
        return pl.pallas_call(
            functools.partial(kernel, step),
            grid_spec=pltpu.PrefetchScalarGridSpec(
                num_scalar_prefetch=1, grid=(blocks,), in_specs=in_specs, out_specs=out_specs
            ),
            out_shape=out_shape,
            compiler_params=pltpu.CompilerParams(vmem_limit_bytes=VMEM_LIMIT),
            cost_estimate=pl.CostEstimate(
                flops=flops * chans * chans * count, bytes_accessed=arrays * chans * 2 * count,
                transcendentals=chans * count,
            ),
        )(flip, *operands)

    def project(part):
        return call(
            project_kernel,
            [row_spec] * 2 + [mask_spec(part)] * 2 + [whole(gain), whole(proj_t)],
            [chan_spec] * 2, [chan_shape] * 2, 8, 3,
            (*pairs[part], *masks, gain, proj_t),
        )

    def middle(comb, part):
        return call(
            middle_kernel,
            [row_spec] * 4 + [chan_spec, whole(gain), whole(gate_t), whole(out_weight), whole(out_t),
                              whole(gain_col), whole(eye)],
            [chan_spec, sigm_spec], [chan_shape, sigm_shape], 8, 5,
            (*pairs[part], *gouts[part], comb, gain, gate_t, out_weight, out_t, gain_col, eye),
        )

    def last(left_grad, right_grad, sigm, part):
        return call(
            last_kernel,
            [row_spec] * 2 + [chan_spec] * 2 + [sigm_spec] + [mask_spec(part)] * 2 + [whole(gain), whole(all_w)],
            [row_spec] * 2, [row_shape] * 2, 18, 5,
            (*pairs[part], left_grad, right_grad, sigm, *masks, gain, all_w),
        )

    def exchange(array):
        return lax.all_to_all(array, GROUP, split_axis=0, concat_axis=0, tiled=True)

    def by_channel(array):
        array = array.reshape(halves, low, row_blocks, halves, rows, own, cols)
        return jnp.transpose(array, (5, 2, 0, 4, 3, 1, 6)).reshape(own, row_blocks, halves, rows, tokens)

    def flat(array):
        return array.reshape(own, -1, tokens)

    def by_owner(array):
        array = array.astype(BF16).reshape(own, row_blocks, halves, rows, halves, low, cols)
        return jnp.transpose(array, (2, 5, 1, 4, 3, 0, 6)).reshape(peers, halves, rows, own, cols)

    def batch_dot(a, b, ca, cb):
        return lax.dot_general(a, b, (((ca,), (cb,)), ((0,), (0,))), preferred_element_type=F32)

    lefts, rights = [], []
    for part in range(chunks):
        left, right = project(part)
        rights.append(by_channel(exchange(right)))
        lefts.append(flat(by_channel(exchange(left))))
    right = flat(jnp.concatenate(rights, axis=3))

    sigms, left_grads, grad_parts = [], [], []
    for part in range(chunks):
        comb = exchange(by_owner(batch_dot(lefts[part], right, 2, 2)))
        grad_comb, sigm = middle(comb, part)
        sigms.append(sigm)
        grad_comb = flat(by_channel(exchange(grad_comb)))
        left_grads.append(exchange(by_owner(batch_dot(grad_comb, right, 2, 1))))
        grad_parts.append(batch_dot(grad_comb, lefts[part], 1, 1))
    grad_right = functools.reduce(jnp.add, grad_parts).astype(BF16)
    grad_right = grad_right.reshape(own, row_blocks, halves, chunks, rows, tokens)

    out = jnp.zeros((full_rows, cols, chans), BF16)
    for part in range(chunks):
        right_grad = exchange(by_owner(grad_right[:, :, :, part]))
        results = last(left_grads[part], right_grad, sigms[part], part)
        for w in range(2):
            home = lax.ppermute(results[w], SWAP, back[w])
            out = lax.dynamic_update_slice_in_dim(out, home, half_of[w] * half_rows + part * rows, 0)
    return out


def solution(mesh):
    size = mesh.shape
    halves = size["rep"]
    split = (size["rep"], halves, size["ch"] // halves, size["row"], size["sub"])
    fine = Mesh(mesh.devices.reshape(split), ("rep", "high", "low", "row", "sub"))
    spread = P(("rep", "row", "sub"), ("high", "low"), None)
    return jax.shard_map(
        functools.partial(local, 2),
        mesh=fine,
        in_specs=(spread, spread, P("rep"), P(), P(), P(), P(), P()),
        out_specs=spread,
        check_vma=False,
    )
```

```python
import functools

import jax
import jax.numpy as jnp
from jax import lax
from jax.experimental import pallas as pl
from jax.experimental.pallas import tpu as pltpu
from jax.sharding import Mesh
from jax.sharding import PartitionSpec as P

epsilon = 1e-05
F32 = jnp.float32
BF16 = jnp.bfloat16
VMEM_LIMIT = 48 * 1024 * 1024
GROUP = ("rep", "low", "row", "sub")
SWAP = ("rep", "high")


def dot(a, b, ca, cb):
    return lax.dot_general(a, b, (((ca,), (cb,)), ((), ())), preferred_element_type=F32)


def norm_rows(pair_block, gain):
    x = pair_block.astype(F32)
    center = x - jnp.mean(x, axis=1, keepdims=True)
    scaled = lax.rsqrt(jnp.mean(center * center, axis=1, keepdims=True) + epsilon)
    hat = center * scaled
    return hat, scaled, (hat * gain).astype(BF16)


def rows_of(ref, first, count):
    block = ref[first:first + count]
    return block.reshape(count * block.shape[1], block.shape[2])


def load_chan(ref, slot, first, count):
    parts = [ref[:, slot, first + t] for t in range(count)]
    parts = [p.astype(F32).reshape(p.shape[0] * p.shape[1], p.shape[2]) for p in parts]
    return parts[0] if count == 1 else jnp.concatenate(parts, axis=1)


def store_chan(ref, slot, first, count, value):
    groups, _, _, chans, cols = ref.shape
    for t in range(count):
        part = value[:, t * cols:(t + 1) * cols] if count > 1 else value
        ref[:, slot, first + t] = part.reshape(groups, chans, cols).astype(BF16)


def project_kernel(step, flip_ref, pair_a, pair_b, mask_a, mask_b, gain_ref, weight_ref, left_ref, right_ref):
    rows, cols, chans = pair_a.shape
    for which, (pair_ref, mask_ref) in enumerate(((pair_a, mask_a), (pair_b, mask_b))):
        slot = flip_ref[which]
        for first in range(0, rows, step):
            _, _, normed = norm_rows(rows_of(pair_ref, first, step), gain_ref[...])
            proj = dot(weight_ref[...], normed, 1, 1)
            mask = mask_ref[0, :, first * cols:(first + step) * cols]
            left = mask * jax.nn.sigmoid(proj[chans:2 * chans]) * proj[:chans]
            right = mask * jax.nn.sigmoid(proj[3 * chans:]) * proj[2 * chans:3 * chans]
            store_chan(left_ref, slot, first, step, left)
            store_chan(right_ref, slot, first, step, right)


def middle_kernel(
    step, flip_ref, pair_a, pair_b, gout_a, gout_b, comb_ref, gain_ref, gate_t_ref, out_w_ref, out_t_ref,
    out_gain_ref, eye_ref, gcomb_ref, sigm_ref,
):
    rows, cols, chans = pair_a.shape
    out_gain = out_gain_ref[...]
    for which, (pair_ref, gout_ref) in enumerate(((pair_a, gout_a), (pair_b, gout_b))):
        slot = flip_ref[which]
        for first in range(0, rows, step):
            _, _, normed = norm_rows(rows_of(pair_ref, first, step), gain_ref[...])
            gate = jax.nn.sigmoid(dot(gate_t_ref[...], normed, 1, 1))
            gout = dot(eye_ref[...], rows_of(gout_ref, first, step), 1, 1)
            comb = load_chan(comb_ref, slot, first, step)
            center = comb - jnp.mean(comb, axis=0, keepdims=True)
            scaled = lax.rsqrt(jnp.mean(center * center, axis=0, keepdims=True) + epsilon)
            hat = center * scaled
            lin = dot(out_t_ref[...], (hat * out_gain).astype(BF16), 1, 0)
            grad_lin = (gout * gate).astype(BF16)
            h = dot(out_w_ref[...], grad_lin, 1, 0) * out_gain
            grad = scaled * (
                h - jnp.mean(h, axis=0, keepdims=True) - hat * jnp.mean(h * hat, axis=0, keepdims=True)
            )
            store_chan(gcomb_ref, slot, first, step, grad)
            sigm = (gout * lin * gate * (1.0 - gate)).astype(BF16)
            for t in range(step):
                sigm_ref[which, first + t] = sigm[:, t * cols:(t + 1) * cols] if step > 1 else sigm


def last_kernel(
    step, flip_ref, pair_a, pair_b, left_ref, right_ref, sigm_ref, mask_a, mask_b, gain_ref, weight_ref, out_a, out_b
):
    rows, cols, chans = pair_a.shape
    gain = gain_ref[...]
    weight = weight_ref[...]
    for which, (pair_ref, mask_ref, out_ref) in enumerate(((pair_a, mask_a, out_a), (pair_b, mask_b, out_b))):
        slot = flip_ref[which]
        for first in range(0, rows, step):
            hat, scaled, normed = norm_rows(rows_of(pair_ref, first, step), gain)
            mask = mask_ref[0, :, first * cols:(first + step) * cols]
            proj = dot(weight[:4 * chans], normed, 1, 1)
            terms = []
            for side, ref in enumerate((left_ref, right_ref)):
                grad = load_chan(ref, slot, first, step) * mask
                value = proj[2 * side * chans:(2 * side + 1) * chans]
                gate = jax.nn.sigmoid(proj[(2 * side + 1) * chans:(2 * side + 2) * chans])
                through = grad * gate
                terms += [through.astype(BF16), (through * value * (1.0 - gate)).astype(BF16)]
            parts = [sigm_ref[which, first + t] for t in range(step)]
            terms.append(parts[0] if step == 1 else jnp.concatenate(parts, axis=1))
            g = dot(jnp.concatenate(terms, axis=0), weight, 0, 0) * gain
            grad_in = scaled * (
                g - jnp.mean(g, axis=1, keepdims=True) - hat * jnp.mean(g * hat, axis=1, keepdims=True)
            )
            out_ref[first:first + step] = grad_in.reshape(step, cols, chans).astype(BF16)


def local(chunks, pair, grad_out, token_mask, ln_gain, proj_weights, gate_weight, out_weight, out_gain):
    full_rows, cols, chans = pair.shape
    halves = lax.axis_size("rep")
    low = lax.axis_size("low")
    row_blocks = lax.axis_size(("row", "sub"))
    peers = halves * low * row_blocks
    own = chans // peers
    tokens = full_rows * row_blocks
    half_rows = full_rows // halves
    rows = half_rows // chunks
    block = min(4, rows)
    blocks = rows // block
    step = 4 if cols % 128 == 0 and block % 4 == 0 else 1
    rep, high = lax.axis_index("rep"), lax.axis_index("high")

    places = [(y, b) for y in range(halves) for b in range(halves)]
    at = {place: n for n, place in enumerate(places)}
    over_rep = [(at[y, b], at[1 - y, b]) for y, b in places]
    over_high = [(at[y, b], at[y, 1 - b]) for y, b in places]
    home = rep == high

    def half_part(array, half, part):
        return lax.dynamic_slice_in_dim(array, half * half_rows + part * rows, rows)

    def swap_rep(array):
        return lax.ppermute(array, SWAP, over_rep)

    def swap_high(array):
        return lax.ppermute(array, SWAP, over_high)

    def first_hop(array, part):
        return swap_rep(half_part(array, 1 - rep, part))

    def second_hop(array, came, part):
        mine = half_part(array, rep, part)
        return jnp.where(home, mine, came), swap_high(jnp.where(home, came, mine))

    def tie(*values):
        return lax.optimization_barrier(values)

    mask_float = token_mask.astype(F32)
    mask_float = jnp.where(home, mask_float, swap_rep(mask_float))

    flip = jnp.stack([high, 1 - high]).astype(jnp.int32)
    row_mask = lax.dynamic_slice_in_dim(
        mask_float, lax.axis_index(("row", "sub")) * full_rows + rep * half_rows, half_rows
    )

    def pair_mask(slot):
        col_mask = lax.dynamic_slice_in_dim(mask_float, (slot * low + lax.axis_index("low")) * cols, cols)
        return (row_mask[:, None] * col_mask[None, :]).reshape(half_rows // block, 1, block * cols)

    masks = [pair_mask(high), pair_mask(1 - high)]
    gain = ln_gain.reshape(1, chans)
    gain_col = out_gain.reshape(chans, 1)
    proj_t = jnp.swapaxes(proj_weights, 1, 2).reshape(4 * chans, chans)
    gate_t = gate_weight.T
    out_t = out_weight.T
    all_w = jnp.concatenate([proj_t, gate_t], axis=0)
    eye = jnp.eye(chans, dtype=BF16)

    row_spec = pl.BlockSpec((block, cols, chans), lambda s, f: (s, 0, 0))
    chan_spec = pl.BlockSpec((peers, halves, block, own, cols), lambda s, f: (0, 0, s, 0, 0))
    sigm_spec = pl.BlockSpec((halves, block, chans, cols), lambda s, f: (0, s, 0, 0))
    row_shape = jax.ShapeDtypeStruct((rows, cols, chans), BF16)
    chan_shape = jax.ShapeDtypeStruct((peers, halves, rows, own, cols), BF16)
    sigm_shape = jax.ShapeDtypeStruct((halves, rows, chans, cols), BF16)

    def mask_spec(part):
        return pl.BlockSpec((1, 1, block * cols), lambda s, f: (part * blocks + s, 0, 0))

    def whole(array):
        return pl.BlockSpec(array.shape, lambda s, f: (0,) * array.ndim)

    def call(kernel, in_specs, out_specs, out_shape, flops, arrays, operands):
        count = halves * rows * cols
        return pl.pallas_call(
            functools.partial(kernel, step),
            grid_spec=pltpu.PrefetchScalarGridSpec(
                num_scalar_prefetch=1, grid=(blocks,), in_specs=in_specs, out_specs=out_specs
            ),
            out_shape=out_shape,
            compiler_params=pltpu.CompilerParams(vmem_limit_bytes=VMEM_LIMIT),
            cost_estimate=pl.CostEstimate(
                flops=flops * chans * chans * count, bytes_accessed=arrays * chans * 2 * count,
                transcendentals=chans * count,
            ),
        )(flip, *operands)

    def project(part):
        return call(
            project_kernel,
            [row_spec] * 2 + [mask_spec(part)] * 2 + [whole(gain), whole(proj_t)],
            [chan_spec] * 2, [chan_shape] * 2, 8, 3,
            (*pairs[part], *masks, gain, proj_t),
        )

    def middle(comb, part):
        return call(
            middle_kernel,
            [row_spec] * 4 + [chan_spec, whole(gain), whole(gate_t), whole(out_weight), whole(out_t),
                              whole(gain_col), whole(eye)],
            [chan_spec, sigm_spec], [chan_shape, sigm_shape], 8, 5,
            (*pairs[part], *gouts[part], comb, gain, gate_t, out_weight, out_t, gain_col, eye),
        )

    def last(left_grad, right_grad, sigm, part):
        return call(
            last_kernel,
            [row_spec] * 2 + [chan_spec] * 2 + [sigm_spec] + [mask_spec(part)] * 2 + [whole(gain), whole(all_w)],
            [row_spec] * 2, [row_shape] * 2, 18, 5,
            (*pairs[part], left_grad, right_grad, sigm, *masks, gain, all_w),
        )

    def exchange(array):
        return lax.all_to_all(array, GROUP, split_axis=0, concat_axis=0, tiled=True)

    def by_channel(array):
        array = array.reshape(halves, low, row_blocks, halves, rows, own, cols)
        return jnp.transpose(array, (5, 2, 0, 4, 3, 1, 6)).reshape(own, row_blocks, halves, rows, tokens)

    def flat(array):
        return array.reshape(own, -1, tokens)

    def by_owner(array):
        array = array.astype(BF16).reshape(own, row_blocks, halves, rows, halves, low, cols)
        return jnp.transpose(array, (2, 5, 1, 4, 3, 0, 6)).reshape(peers, halves, rows, own, cols)

    def batch_dot(a, b, ca, cb):
        return lax.dot_general(a, b, (((ca,), (cb,)), ((0,), (0,))), preferred_element_type=F32)

    pairs, gouts = [None] * chunks, [None] * chunks
    came = first_hop(pair, 0)
    later, came = tie(pair, came)
    pairs[0] = second_hop(pair, came, 0)
    came = first_hop(later, 1)
    (*pairs[0], came) = tie(*pairs[0], came)
    left_a, right_a = project(0)
    right_a = exchange(right_a)
    pairs[1] = second_hop(pair, came, 1)
    (left_a, *pairs[1]) = tie(left_a, *pairs[1])
    left_a = exchange(left_a)
    later, right_a = tie(grad_out, right_a)
    came = first_hop(later, 0)
    left_b, right_b = project(1)
    right_b, came = tie(right_b, came)
    right_b = exchange(right_b)
    gouts[0] = second_hop(grad_out, came, 0)
    (left_b, *gouts[0]) = tie(left_b, *gouts[0])
    left_b = exchange(left_b)
    later, right_b = tie(later, right_b)
    came = first_hop(later, 1)
    right = flat(jnp.concatenate([by_channel(right_a), by_channel(right_b)], axis=3))
    lefts = [flat(by_channel(left_a)), flat(by_channel(left_b))]
    comb_a = by_owner(batch_dot(lefts[0], right, 2, 2))
    comb_a, came = tie(comb_a, came)
    comb_a = exchange(comb_a)
    gouts[1] = second_hop(grad_out, came, 1)
    comb_b = by_owner(batch_dot(lefts[1], right, 2, 2))
    (comb_b, *gouts[1]) = tie(comb_b, *gouts[1])
    combs = [comb_a, exchange(comb_b)]

    sigms, left_grads, grad_parts = [], [], []
    for part in range(chunks):
        grad_comb, sigm = middle(combs[part], part)
        sigms.append(sigm)
        grad_comb = flat(by_channel(exchange(grad_comb)))
        left_grads.append(exchange(by_owner(batch_dot(grad_comb, right, 2, 1))))
        grad_parts.append(batch_dot(grad_comb, lefts[part], 1, 1))
    grad_right = functools.reduce(jnp.add, grad_parts).astype(BF16)
    grad_right = grad_right.reshape(own, row_blocks, halves, chunks, rows, tokens)

    out = jnp.zeros((full_rows, cols, chans), BF16)
    for part in range(chunks):
        right_grad = exchange(by_owner(grad_right[:, :, :, part]))
        kept, goes = last(left_grads[part], right_grad, sigms[part], part)
        came = swap_high(goes)
        stays, goes = jnp.where(home, kept, came), jnp.where(home, came, kept)
        came = swap_rep(goes)
        out = lax.dynamic_update_slice_in_dim(out, stays, rep * half_rows + part * rows, 0)
        out = lax.dynamic_update_slice_in_dim(out, came, (1 - rep) * half_rows + part * rows, 0)
    return out


def solution(mesh):
    size = mesh.shape
    halves = size["rep"]
    split = (size["rep"], halves, size["ch"] // halves, size["row"], size["sub"])
    fine = Mesh(mesh.devices.reshape(split), ("rep", "high", "low", "row", "sub"))
    spread = P(("rep", "row", "sub"), ("high", "low"), None)
    return jax.shard_map(
        functools.partial(local, 2),
        mesh=fine,
        in_specs=(spread, spread, P("rep"), P(), P(), P(), P(), P()),
        out_specs=spread,
        check_vma=False,
    )
```

```python
import functools

import jax
import jax.numpy as jnp
from jax import lax
from jax.experimental import pallas as pl
from jax.experimental.pallas import tpu as pltpu
from jax.sharding import PartitionSpec as P

epsilon = 1e-05
F32 = jnp.float32
BF16 = jnp.bfloat16
VMEM_LIMIT = 48 * 1024 * 1024


def dot(a, b, ca, cb):
    return lax.dot_general(a, b, (((ca,), (cb,)), ((), ())), preferred_element_type=F32)


def norm_rows(pair_block, gain):
    x = pair_block.astype(F32)
    center = x - jnp.mean(x, axis=1, keepdims=True)
    scaled = lax.rsqrt(jnp.mean(center * center, axis=1, keepdims=True) + epsilon)
    hat = center * scaled
    return hat, scaled, (hat * gain).astype(BF16)


def rows_of(ref, first, count):
    block = ref[first:first + count]
    return block.reshape(count * block.shape[1], block.shape[2])


def load_chan(ref, first, count):
    parts = [ref[:, first + t] for t in range(count)]
    parts = [p.astype(F32).reshape(p.shape[0] * p.shape[1], p.shape[2]) for p in parts]
    return parts[0] if count == 1 else jnp.concatenate(parts, axis=1)


def store_chan(ref, first, count, value):
    groups, _, chans, cols = ref.shape
    for t in range(count):
        part = value[:, t * cols:(t + 1) * cols] if count > 1 else value
        ref[:, first + t] = part.reshape(groups, chans, cols).astype(BF16)


def project_kernel(step, pair_ref, mask_ref, gain_ref, weight_ref, out_ref):
    rows, cols, chans = pair_ref.shape
    for first in range(0, rows, step):
        _, _, normed = norm_rows(rows_of(pair_ref, first, step), gain_ref[...])
        both = dot(weight_ref[0], normed, 1, 1)
        mask = mask_ref[0, :, first * cols:(first + step) * cols]
        store_chan(out_ref, first, step, mask * jax.nn.sigmoid(both[chans:]) * both[:chans])


def middle_kernel(
    step, pair_ref, gout_ref, comb_ref, gain_ref, gate_t_ref, out_w_ref, out_t_ref, out_gain_ref, eye_ref,
    gcomb_ref, sigm_ref,
):
    rows, cols, chans = pair_ref.shape
    out_gain = out_gain_ref[...]
    for first in range(0, rows, step):
        _, _, normed = norm_rows(rows_of(pair_ref, first, step), gain_ref[...])
        gate = jax.nn.sigmoid(dot(gate_t_ref[...], normed, 1, 1))
        gout = dot(eye_ref[...], rows_of(gout_ref, first, step), 1, 1)
        comb = load_chan(comb_ref, first, step)
        center = comb - jnp.mean(comb, axis=0, keepdims=True)
        scaled = lax.rsqrt(jnp.mean(center * center, axis=0, keepdims=True) + epsilon)
        hat = center * scaled
        lin = dot(out_t_ref[...], (hat * out_gain).astype(BF16), 1, 0)
        grad_lin = (gout * gate).astype(BF16)
        h = dot(out_w_ref[...], grad_lin, 1, 0) * out_gain
        grad = scaled * (
            h - jnp.mean(h, axis=0, keepdims=True) - hat * jnp.mean(h * hat, axis=0, keepdims=True)
        )
        store_chan(gcomb_ref, first, step, grad)
        sigm = (gout * lin * gate * (1.0 - gate)).astype(BF16)
        for t in range(step):
            sigm_ref[first + t] = sigm[:, t * cols:(t + 1) * cols] if step > 1 else sigm


def last_kernel(
    step, pair_ref, left_ref, right_ref, sigm_ref, mask_ref, gain_ref, weight_ref, held_ref, out_ref
):
    del held_ref
    rows, cols, chans = pair_ref.shape
    gain = gain_ref[...]
    weight = weight_ref[...]
    for first in range(0, rows, step):
        hat, scaled, normed = norm_rows(rows_of(pair_ref, first, step), gain)
        mask = mask_ref[0, :, first * cols:(first + step) * cols]
        proj = dot(weight[:4 * chans], normed, 1, 1)
        terms = []
        for which, ref in enumerate((left_ref, right_ref)):
            grad = load_chan(ref, first, step) * mask
            value = proj[2 * which * chans:(2 * which + 1) * chans]
            gate = jax.nn.sigmoid(proj[(2 * which + 1) * chans:(2 * which + 2) * chans])
            through = grad * gate
            terms += [through.astype(BF16), (through * value * (1.0 - gate)).astype(BF16)]
        parts = [sigm_ref[first + t] for t in range(step)]
        terms.append(parts[0] if step == 1 else jnp.concatenate(parts, axis=1))
        g = dot(jnp.concatenate(terms, axis=0), weight, 0, 0) * gain
        grad_in = scaled * (
            g - jnp.mean(g, axis=1, keepdims=True) - hat * jnp.mean(g * hat, axis=1, keepdims=True)
        )
        out_ref[first:first + step] = grad_in.reshape(step, cols, chans).astype(BF16)


def local(group, chunks, pair, grad_out, token_mask, ln_gain, proj_weights, gate_weight, out_weight, out_gain):
    rows, cols, chans = pair.shape
    peers = lax.axis_size(group)
    row_blocks = lax.axis_size(group[1:])
    col_blocks = peers // row_blocks
    own = chans // peers
    tokens = rows * row_blocks
    part_rows = rows // chunks
    block = min(8, part_rows)
    blocks = part_rows // block
    step = 4 if cols % 128 == 0 and block % 4 == 0 else 1

    mask_float = token_mask.astype(F32)
    row_mask = lax.dynamic_slice_in_dim(mask_float, lax.axis_index(group[1:]) * rows, rows)
    col_mask = lax.dynamic_slice_in_dim(mask_float, lax.axis_index(group[0]) * cols, cols)
    mask = (row_mask[:, None] * col_mask[None, :]).reshape(rows // block, 1, block * cols)
    gain = ln_gain.reshape(1, chans)
    proj_t = jnp.swapaxes(proj_weights, 1, 2)
    sides = proj_t.reshape(2, 2 * chans, chans)
    gate_t = gate_weight.T
    all_w = jnp.concatenate([proj_t.reshape(4 * chans, chans), gate_t], axis=0)
    eye = jnp.eye(chans, dtype=BF16)

    params = pltpu.CompilerParams(vmem_limit_bytes=VMEM_LIMIT)

    def cost(flops_per_pair, arrays, pairs):
        return pl.CostEstimate(
            flops=flops_per_pair * pairs, bytes_accessed=arrays * pairs * chans * 2, transcendentals=chans * pairs
        )

    def row_spec(first):
        return pl.BlockSpec((block, cols, chans), lambda s: (first + s, 0, 0))

    def mask_spec(first):
        return pl.BlockSpec((1, 1, block * cols), lambda s: (first + s, 0, 0))

    def whole(array):
        return pl.BlockSpec(array.shape, lambda s: (0,) * array.ndim)

    chan_spec = pl.BlockSpec((peers, block, own, cols), lambda s: (0, s, 0, 0))
    sigm_spec = pl.BlockSpec((block, chans, cols), lambda s: (s, 0, 0))

    def project(rights, first, count):
        def place(s):
            return jnp.where(s < rights, s, s - rights + first)

        return pl.pallas_call(
            functools.partial(project_kernel, step),
            grid=(rights + count,),
            in_specs=[
                pl.BlockSpec((block, cols, chans), lambda s: (place(s), 0, 0)),
                pl.BlockSpec((1, 1, block * cols), lambda s: (place(s), 0, 0)),
                whole(gain),
                pl.BlockSpec((1, 2 * chans, chans), lambda s: (jnp.where(s < rights, 1, 0), 0, 0)),
            ],
            out_specs=chan_spec,
            out_shape=jax.ShapeDtypeStruct((peers, (rights + count) * block, own, cols), BF16),
            compiler_params=params,
            cost_estimate=cost(4 * chans * chans, 2, (rights + count) * block * cols),
        )(pair, mask, gain, sides)

    def exchange(array):
        return lax.all_to_all(array, group, split_axis=0, concat_axis=0, tiled=True)

    def by_channel(array):
        count = array.shape[1]
        array = array.reshape(col_blocks, row_blocks, count, own, cols)
        return jnp.transpose(array, (3, 1, 2, 0, 4)).reshape(own, row_blocks * count, tokens)

    def by_owner(array):
        count = array.shape[1] // row_blocks
        array = array.astype(BF16).reshape(own, row_blocks, count, col_blocks, cols)
        return jnp.transpose(array, (3, 1, 2, 0, 4)).reshape(peers, count, own, cols)

    def batch_dot(a, b, ca, cb):
        return lax.dot_general(a, b, (((ca,), (cb,)), ((0,), (0,))), preferred_element_type=F32)

    def middle(comb, first):
        out_t = out_weight.T
        gain_col = out_gain.reshape(chans, 1)
        return pl.pallas_call(
            functools.partial(middle_kernel, step),
            grid=(blocks,),
            in_specs=[row_spec(first), row_spec(first), chan_spec, whole(gain), whole(gate_t), whole(out_weight),
                      whole(out_t), whole(gain_col), whole(eye)],
            out_specs=[chan_spec, sigm_spec],
            out_shape=[
                jax.ShapeDtypeStruct((peers, part_rows, own, cols), BF16),
                jax.ShapeDtypeStruct((part_rows, chans, cols), BF16),
            ],
            compiler_params=params,
            cost_estimate=cost(8 * chans * chans, 5, part_rows * cols),
        )(pair, grad_out, comb, gain, gate_t, out_weight, out_t, gain_col, eye)

    def chan_from(first):
        return pl.BlockSpec((peers, block, own, cols), lambda s: (0, first + s, 0, 0))

    def last(left_grad, right_grad, sigm, first, held):
        (left_grad, left_at), (right_grad, right_at) = left_grad, right_grad
        return pl.pallas_call(
            functools.partial(last_kernel, step),
            grid=(blocks,),
            in_specs=[row_spec(first), chan_from(left_at), chan_from(right_at), sigm_spec, mask_spec(first), whole(gain), whole(all_w),
                      pl.BlockSpec(memory_space=pl.ANY)],
            out_specs=row_spec(first),
            out_shape=jax.ShapeDtypeStruct((rows, cols, chans), BF16),
            input_output_aliases={7: 0},
            compiler_params=params,
            cost_estimate=cost(18 * chans * chans, 5, part_rows * cols),
        )(pair, left_grad, right_grad, sigm, mask, gain, all_w, held)

    firsts = [part * blocks for part in range(chunks)]
    both = exchange(project(rows // block, 0, blocks))
    right = by_channel(both[:, :rows])
    lefts = [by_channel(both[:, rows:])]
    lefts += [by_channel(exchange(project(0, first, blocks))) for first in firsts[1:]]
    sigms, left_grads, grad_parts = [], [], []
    for first, left in zip(firsts, lefts):
        comb = exchange(by_owner(batch_dot(left, right, 2, 2)))
        grad_comb, sigm = middle(comb, first)
        sigms.append(sigm)
        grad_comb = by_channel(exchange(grad_comb))
        left_grads.append(by_owner(batch_dot(grad_comb, right, 2, 1)))
        grad_parts.append(batch_dot(grad_comb, left, 1, 1))
    grad_right = by_owner(functools.reduce(jnp.add, grad_parts))
    right_grads = [grad_right[:, p * part_rows:(p + 1) * part_rows] for p in range(chunks)]
    left_sent = [(exchange(array), 0) for array in left_grads[:-1]]
    both = exchange(jnp.concatenate([left_grads[-1], right_grads[0]], axis=1))
    left_sent.append((both, 0))
    right_sent = [(both, blocks)] + [(exchange(array), 0) for array in right_grads[1:]]
    out = jnp.zeros((rows, cols, chans), BF16)
    for first, left_grad, right_grad, sigm in zip(firsts, left_sent, right_sent, sigms):
        out = last(left_grad, right_grad, sigm, first, out)
    return out


def solution(mesh):
    spread = P(("rep", "row", "sub"), "ch", None)
    return jax.shard_map(
        functools.partial(local, ("ch", "row", "sub"), 2),
        mesh=mesh,
        in_specs=(spread, spread, P("rep"), P(), P(), P(), P(), P()),
        out_specs=spread,
        check_vma=False,
    )
```

```python
import functools

import jax
import jax.numpy as jnp
from jax import lax
from jax.experimental import pallas as pl
from jax.experimental.pallas import tpu as pltpu
from jax.sharding import PartitionSpec as P

epsilon = 1e-05
F32 = jnp.float32
BF16 = jnp.bfloat16
VMEM_LIMIT = 56 * 1024 * 1024
ROWS = ("row", "sub")


def dot(a, b, ca, cb):
    return lax.dot_general(a, b, (((ca,), (cb,)), ((), ())), preferred_element_type=F32)


def turn(block):
    return jnp.swapaxes(block.astype(F32), 0, 1)


def norm_rows(pair_block, gain):
    x = pair_block.astype(F32)
    center = x - jnp.mean(x, axis=1, keepdims=True)
    scaled = lax.rsqrt(jnp.mean(center * center, axis=1, keepdims=True) + epsilon)
    hat = center * scaled
    return hat, scaled, (hat * gain).astype(BF16)


def rows_of(ref, first, count):
    block = ref[first:first + count]
    return block.reshape(count * block.shape[1], block.shape[2])


def load_chan(refs, first, count):
    parts = [jnp.concatenate([ref[first + t].astype(F32) for ref in refs], axis=0) for t in range(count)]
    return parts[0] if count == 1 else jnp.concatenate(parts, axis=1)


def store_chan(refs, first, count, value):
    _, own, cols = refs[0].shape
    for s, ref in enumerate(refs):
        group = value[s * own:(s + 1) * own].astype(BF16)
        for t in range(count):
            ref[first + t] = group[:, t * cols:(t + 1) * cols] if count > 1 else group


def project_kernel(step, pair_ref, mask_ref, gain_ref, weight_ref, *out_refs):
    rows, cols, chans = pair_ref.shape
    for first in range(0, rows, step):
        _, _, normed = norm_rows(rows_of(pair_ref, first, step), gain_ref[...])
        both = dot(weight_ref[...], normed, 1, 1)
        mask = mask_ref[0, :, first * cols:(first + step) * cols]
        store_chan(out_refs, first, step, mask * jax.nn.sigmoid(both[chans:]) * both[:chans])


def middle_kernel(
    step, groups, pair_ref, gout_ref, gain_ref, gate_t_ref, out_w_ref, out_t_ref, out_gain_ref, eye_ref, *refs
):
    comb_refs, gcomb_refs, sigm_ref = refs[:groups], refs[groups:2 * groups], refs[2 * groups]
    rows, cols, chans = pair_ref.shape
    out_gain = out_gain_ref[...]
    for first in range(0, rows, step):
        _, _, normed = norm_rows(rows_of(pair_ref, first, step), gain_ref[...])
        gate = jax.nn.sigmoid(dot(gate_t_ref[...], normed, 1, 1))
        gout = dot(eye_ref[...], rows_of(gout_ref, first, step), 1, 1)
        comb = load_chan(comb_refs, first, step)
        center = comb - jnp.mean(comb, axis=0, keepdims=True)
        scaled = lax.rsqrt(jnp.mean(center * center, axis=0, keepdims=True) + epsilon)
        hat = center * scaled
        lin = dot(out_t_ref[...], (hat * out_gain).astype(BF16), 1, 0)
        grad_lin = (gout * gate).astype(BF16)
        h = dot(out_w_ref[...], grad_lin, 1, 0) * out_gain
        grad = scaled * (
            h - jnp.mean(h, axis=0, keepdims=True) - hat * jnp.mean(h * hat, axis=0, keepdims=True)
        )
        store_chan(gcomb_refs, first, step, grad)
        sigm = (gout * lin * gate * (1.0 - gate)).astype(BF16)
        for t in range(step):
            sigm_ref[first + t] = sigm[:, t * cols:(t + 1) * cols] if step > 1 else sigm


def last_kernel(step, groups, pair_ref, sigm_ref, mask_ref, gain_ref, weight_ref, held_ref, *refs):
    del held_ref
    left_refs, right_refs, out_ref = refs[:groups], refs[groups:2 * groups], refs[2 * groups]
    rows, cols, chans = pair_ref.shape
    gain = gain_ref[...]
    weight = weight_ref[...]
    for first in range(0, rows, step):
        hat, scaled, normed = norm_rows(rows_of(pair_ref, first, step), gain)
        mask = mask_ref[0, :, first * cols:(first + step) * cols]
        proj = dot(weight[:4 * chans], normed, 1, 1)
        terms = []
        for which, piece_refs in enumerate((left_refs, right_refs)):
            grad = load_chan(piece_refs, first, step) * mask
            value = proj[2 * which * chans:(2 * which + 1) * chans]
            gate = jax.nn.sigmoid(proj[(2 * which + 1) * chans:(2 * which + 2) * chans])
            through = grad * gate
            terms += [through.astype(BF16), (through * value * (1.0 - gate)).astype(BF16)]
        parts = [sigm_ref[first + t] for t in range(step)]
        terms.append(parts[0] if step == 1 else jnp.concatenate(parts, axis=1))
        g = dot(jnp.concatenate(terms, axis=0), weight, 0, 0) * gain
        grad_in = scaled * (
            g - jnp.mean(g, axis=1, keepdims=True) - hat * jnp.mean(g * hat, axis=1, keepdims=True)
        )
        out_ref[first:first + step] = grad_in.reshape(step, cols, chans).astype(BF16)


def gather_kernel(*refs):
    out_ref = refs[-1]
    blocks, _, cols, _ = out_ref.shape
    for s, ref in enumerate(refs[:-1]):
        turned = turn(ref[...]).astype(BF16)
        for b in range(blocks):
            out_ref[b, :, :, s * cols:(s + 1) * cols] = turned[:, b * cols:(b + 1) * cols]


def split_kernel(in_ref, *out_refs):
    cols = out_refs[0].shape[2]
    for s, ref in enumerate(out_refs):
        ref[...] = turn(in_ref[0, :, :, s * cols:(s + 1) * cols]).astype(BF16)


def combine_kernel(groups, partner_ref, right_ref, *refs):
    left_refs, out_refs, left_buf, sums = refs[:groups], refs[groups:2 * groups], refs[2 * groups], refs[-1]
    rows, own, cols = left_refs[0].shape
    for s, ref in enumerate(left_refs):
        left_buf[:, :, s * cols:(s + 1) * cols] = turn(ref[...]).astype(BF16)
    for s, ref in enumerate(out_refs):
        other = partner_ref[s]
        for c in range(own):
            sums[c] = dot(left_buf[c], right_ref[other, c], 1, 1)
        ref[...] = turn(sums[...]).astype(BF16)


def left_kernel(groups, partner_ref, right_ref, *refs):
    grad_refs, out_refs, sums = refs[:groups], refs[groups:2 * groups], refs[-1]
    rows, own, cols = grad_refs[0].shape
    grads = [turn(ref[...]).astype(BF16) for ref in grad_refs]
    for c in range(own):
        total = dot(grads[0][c], right_ref[partner_ref[0], c], 1, 0)
        for s in range(1, groups):
            total += dot(grads[s][c], right_ref[partner_ref[s], c], 1, 0)
        sums[c] = total
    for s, ref in enumerate(out_refs):
        ref[...] = turn(sums[:, :, s * cols:(s + 1) * cols]).astype(BF16)


def right_kernel(groups, chunks, partner_ref, *refs):
    count = groups * chunks
    grad_refs, left_refs, out_refs, left_buf = refs[:count], refs[count:2 * count], refs[2 * count:-1], refs[-1]
    rows, own, cols = grad_refs[0].shape
    part = out_refs[0].shape[2]
    row_blocks = out_refs[0].shape[0]
    span = groups // row_blocks
    for n, ref in enumerate(left_refs):
        piece, s = divmod(n, groups)
        left_buf[:, piece * rows:(piece + 1) * rows, s * cols:(s + 1) * cols] = turn(ref[...]).astype(BF16)
    for s in range(groups):
        grads = [turn(grad_refs[piece * groups + s][...]).astype(BF16) for piece in range(chunks)]
        grad = grads[0] if chunks == 1 else jnp.concatenate(grads, axis=1)
        other = partner_ref[s]
        owner = other // span
        for c in range(own):
            total = dot(grad[c], left_buf[c], 0, 0).astype(BF16)
            for m in range(cols // part):
                block = total[m * part:(m + 1) * part]
                if span == 1:
                    out_refs[m][owner, c] = block
                else:
                    chunk = (other % span) * (cols // part) + m
                    for h, ref in enumerate(out_refs):

                        @pl.when(chunk == h)
                        def _(ref=ref, block=block, c=c):
                            ref[owner, c] = block


def local(chunks, pair, grad_out, token_mask, ln_gain, proj_weights, gate_weight, out_weight, out_gain):
    rows, cols, chans = pair.shape
    groups = lax.axis_size("ch")
    row_blocks = lax.axis_size(ROWS)
    own = chans // groups
    tokens = rows * row_blocks
    part_rows = rows // chunks
    block = min(8, part_rows)
    blocks = part_rows // block
    step = 4 if cols % 128 == 0 and block % 4 == 0 else 1
    some = 16 if own % 16 == 0 else own
    z = lax.axis_index("ch")
    partner = jnp.stack([z ^ s for s in range(groups)]).astype(jnp.int32)

    def mine(array, axis):
        parts = [lax.dynamic_slice_in_dim(array, (z ^ s) * own, own, axis) for s in range(groups)]
        return jnp.concatenate(parts, axis=axis)

    mask_float = token_mask.astype(F32)
    row_mask = lax.dynamic_slice_in_dim(mask_float, lax.axis_index(ROWS) * rows, rows)
    col_mask = lax.dynamic_slice_in_dim(mask_float, z * cols, cols)
    mask = (row_mask[:, None] * col_mask[None, :]).reshape(rows // block, 1, block * cols)
    gain = ln_gain.reshape(1, chans)
    proj_t = mine(jnp.swapaxes(proj_weights, 1, 2), 1)
    left_w = proj_t[:2].reshape(2 * chans, chans)
    right_w = proj_t[2:].reshape(2 * chans, chans)
    gate_t = gate_weight.T
    all_w = jnp.concatenate([left_w, right_w, gate_t], axis=0)
    out_w = mine(out_weight, 0)
    out_t = out_w.T
    gain_col = mine(out_gain, 0).reshape(chans, 1)
    eye = jnp.eye(chans, dtype=BF16)

    params = pltpu.CompilerParams(vmem_limit_bytes=VMEM_LIMIT)

    def cost(flops, arrays):
        return pl.CostEstimate(
            flops=flops, bytes_accessed=arrays * part_rows * cols * chans * 2, transcendentals=0
        )

    pairs = part_rows * cols

    def row_spec(first):
        return pl.BlockSpec((block, cols, chans), lambda s: (first + s, 0, 0))

    def mask_spec(first):
        return pl.BlockSpec((1, 1, block * cols), lambda s: (first + s, 0, 0))

    def whole(array):
        return pl.BlockSpec(array.shape, lambda s: (0,) * array.ndim)

    piece_spec = pl.BlockSpec((block, own, cols), lambda s: (s, 0, 0))
    sigm_spec = pl.BlockSpec((block, chans, cols), lambda s: (s, 0, 0))

    def pieces(count):
        return [jax.ShapeDtypeStruct((count, own, cols), BF16)] * groups

    def project(weight, first, count):
        return pl.pallas_call(
            functools.partial(project_kernel, step),
            grid=(count,),
            in_specs=[row_spec(first), mask_spec(first), whole(gain), whole(weight)],
            out_specs=[piece_spec] * groups,
            out_shape=pieces(count * block),
            compiler_params=params,
            cost_estimate=cost(4 * chans * chans * count * block * cols, 2 * count // blocks),
        )(pair, mask, gain, weight)

    def middle(comb, first):
        return pl.pallas_call(
            functools.partial(middle_kernel, step, groups),
            grid=(blocks,),
            in_specs=[row_spec(first), row_spec(first), whole(gain), whole(gate_t), whole(out_w),
                      whole(out_t), whole(gain_col), whole(eye)] + [piece_spec] * groups,
            out_specs=[piece_spec] * groups + [sigm_spec],
            out_shape=pieces(part_rows) + [jax.ShapeDtypeStruct((part_rows, chans, cols), BF16)],
            compiler_params=params,
            cost_estimate=cost(8 * chans * chans * pairs, 5),
        )(pair, grad_out, gain, gate_t, out_w, out_t, gain_col, eye, *comb)

    def last(left_grad, right_grad, sigm, first, held):
        return pl.pallas_call(
            functools.partial(last_kernel, step, groups),
            grid=(blocks,),
            in_specs=[row_spec(first), sigm_spec, mask_spec(first), whole(gain), whole(all_w),
                      pl.BlockSpec(memory_space=pl.ANY)] + [piece_spec] * (2 * groups),
            out_specs=row_spec(first),
            out_shape=jax.ShapeDtypeStruct((rows, cols, chans), BF16),
            input_output_aliases={5: 0},
            compiler_params=params,
            cost_estimate=cost(18 * chans * chans * pairs, 5),
        )(pair, sigm, mask, gain, all_w, held, *left_grad, *right_grad)

    def exchange(sent):
        return [sent[0]] + [
            lax.ppermute(sent[s], "ch", [(a, a ^ s) for a in range(groups)]) for s in range(1, groups)
        ]

    def chan_spec(count):
        return pl.BlockSpec((count, some, cols), lambda g, *_: (0, g, 0))

    def all_spec(*shape):
        lead, tail = shape[0], shape[1:]
        return pl.BlockSpec((lead, some) + tail, lambda g, *_: (0, g, 0, 0))

    def gather(got):
        return pl.pallas_call(
            gather_kernel,
            grid=(own // some,),
            in_specs=[chan_spec(rows)] * groups,
            out_specs=all_spec(rows // cols, cols, tokens),
            out_shape=jax.ShapeDtypeStruct((rows // cols, own, cols, tokens), BF16),
            compiler_params=params,
            cost_estimate=cost(0, 4),
        )(*got)

    def split(array):
        return pl.pallas_call(
            split_kernel,
            grid=(own // some,),
            in_specs=[all_spec(1, part_rows, tokens)],
            out_specs=[chan_spec(part_rows)] * groups,
            out_shape=pieces(part_rows),
            compiler_params=params,
            cost_estimate=cost(0, 2),
        )(array)

    product = 2 * part_rows * tokens * tokens * own

    def with_right(kernel, got, scratch):
        return pl.pallas_call(
            functools.partial(kernel, groups),
            grid_spec=pltpu.PrefetchScalarGridSpec(
                num_scalar_prefetch=1, grid=(own // some,),
                in_specs=[all_spec(groups, cols, tokens)] + [chan_spec(part_rows)] * groups,
                out_specs=[chan_spec(part_rows)] * groups,
                scratch_shapes=scratch,
            ),
            out_shape=pieces(part_rows),
            compiler_params=params,
            cost_estimate=cost(product, 2 + row_blocks * chunks),
        )(partner, right, *got)

    def combine(left):
        return with_right(combine_kernel, left, [
            pltpu.VMEM((some, part_rows, tokens), BF16), pltpu.VMEM((some, part_rows, cols), F32)
        ])

    def left_back(grad):
        return with_right(left_kernel, grad, [pltpu.VMEM((some, part_rows, tokens), F32)])

    def right_back(grads, lefts):
        return pl.pallas_call(
            functools.partial(right_kernel, groups, chunks),
            grid_spec=pltpu.PrefetchScalarGridSpec(
                num_scalar_prefetch=1, grid=(own // some,),
                in_specs=[chan_spec(part_rows)] * (2 * groups * chunks),
                out_specs=[all_spec(row_blocks, part_rows, tokens)] * chunks,
                scratch_shapes=[pltpu.VMEM((some, rows, tokens), BF16)],
            ),
            out_shape=[jax.ShapeDtypeStruct((row_blocks, own, part_rows, tokens), BF16)] * chunks,
            compiler_params=params,
            cost_estimate=cost(product * chunks, (2 + row_blocks) * chunks),
        )(partner, *sum(grads, []), *sum(lefts, []))

    firsts = [p * blocks for p in range(chunks)]
    right = gather(exchange(project(right_w, 0, rows // block)))
    right = lax.all_gather(right, ROWS, axis=0, tiled=True)
    lefts = [exchange(project(left_w, first, blocks)) for first in firsts]
    sigms, left_grads, grads = [], [], []
    for first, left in zip(firsts, lefts):
        *grad_comb, sigm = middle(exchange(combine(left)), first)
        sigms.append(sigm)
        grads.append(exchange(grad_comb))
        left_grads.append(exchange(left_back(grads[-1])))
    right_grads = [
        exchange(split(lax.psum_scatter(array, ROWS, scatter_dimension=0, tiled=True)))
        for array in right_back(grads, lefts)
    ]
    out = jnp.zeros((rows, cols, chans), BF16)
    for first, left_grad, right_grad, sigm in zip(firsts, left_grads, right_grads, sigms):
        out = last(left_grad, right_grad, sigm, first, out)
    return out


def solution(mesh):
    spread = P(("rep", "row", "sub"), "ch", None)
    return jax.shard_map(
        functools.partial(local, 2),
        mesh=mesh,
        in_specs=(spread, spread, P("rep"), P(), P(), P(), P(), P()),
        out_specs=spread,
        check_vma=False,
    )
```

```python
import functools

import jax
import jax.numpy as jnp
from jax import lax
from jax.experimental import pallas as pl
from jax.experimental.pallas import tpu as pltpu
from jax.sharding import PartitionSpec as P

epsilon = 1e-05
F32 = jnp.float32
BF16 = jnp.bfloat16
VMEM_LIMIT = 56 * 1024 * 1024
ROWS = ("row", "sub")


def dot(a, b, ca, cb):
    return lax.dot_general(a, b, (((ca,), (cb,)), ((), ())), preferred_element_type=F32)


def turn(block):
    return jnp.swapaxes(block.astype(F32), 0, 1)


def norm_rows(pair_block, gain):
    x = pair_block.astype(F32)
    center = x - jnp.mean(x, axis=1, keepdims=True)
    scaled = lax.rsqrt(jnp.mean(center * center, axis=1, keepdims=True) + epsilon)
    hat = center * scaled
    return hat, scaled, (hat * gain).astype(BF16)


def rows_of(ref, first, count):
    block = ref[first:first + count]
    return block.reshape(count * block.shape[1], block.shape[2])


def load_chan(refs, first, count):
    parts = [jnp.concatenate([ref[first + t].astype(F32) for ref in refs], axis=0) for t in range(count)]
    return parts[0] if count == 1 else jnp.concatenate(parts, axis=1)


def store_chan(refs, first, count, value):
    _, own, cols = refs[0].shape
    for s, ref in enumerate(refs):
        group = value[s * own:(s + 1) * own].astype(BF16)
        for t in range(count):
            ref[first + t] = group[:, t * cols:(t + 1) * cols] if count > 1 else group


def project_kernel(step, pair_ref, mask_ref, gain_ref, weight_ref, *out_refs):
    rows, cols, chans = pair_ref.shape
    for first in range(0, rows, step):
        _, _, normed = norm_rows(rows_of(pair_ref, first, step), gain_ref[...])
        both = dot(weight_ref[...], normed, 1, 1)
        mask = mask_ref[0, :, first * cols:(first + step) * cols]
        store_chan(out_refs, first, step, mask * jax.nn.sigmoid(both[chans:]) * both[:chans])


def middle_kernel(
    step, groups, pair_ref, gout_ref, gain_ref, gate_t_ref, out_w_ref, out_t_ref, out_gain_ref, eye_ref, *refs
):
    comb_refs, gcomb_refs, sigm_ref = refs[:groups], refs[groups:2 * groups], refs[2 * groups]
    rows, cols, chans = pair_ref.shape
    out_gain = out_gain_ref[...]
    for first in range(0, rows, step):
        _, _, normed = norm_rows(rows_of(pair_ref, first, step), gain_ref[...])
        gate = jax.nn.sigmoid(dot(gate_t_ref[...], normed, 1, 1))
        gout = dot(eye_ref[...], rows_of(gout_ref, first, step), 1, 1)
        comb = load_chan(comb_refs, first, step)
        center = comb - jnp.mean(comb, axis=0, keepdims=True)
        scaled = lax.rsqrt(jnp.mean(center * center, axis=0, keepdims=True) + epsilon)
        hat = center * scaled
        lin = dot(out_t_ref[...], (hat * out_gain).astype(BF16), 1, 0)
        grad_lin = (gout * gate).astype(BF16)
        h = dot(out_w_ref[...], grad_lin, 1, 0) * out_gain
        grad = scaled * (
            h - jnp.mean(h, axis=0, keepdims=True) - hat * jnp.mean(h * hat, axis=0, keepdims=True)
        )
        store_chan(gcomb_refs, first, step, grad)
        sigm = (gout * lin * gate * (1.0 - gate)).astype(BF16)
        for t in range(step):
            sigm_ref[first + t] = sigm[:, t * cols:(t + 1) * cols] if step > 1 else sigm


def last_kernel(step, groups, pair_ref, sigm_ref, mask_ref, gain_ref, weight_ref, held_ref, *refs):
    del held_ref
    left_refs, right_refs, out_ref = refs[:groups], refs[groups:2 * groups], refs[2 * groups]
    rows, cols, chans = pair_ref.shape
    gain = gain_ref[...]
    weight = weight_ref[...]
    for first in range(0, rows, step):
        hat, scaled, normed = norm_rows(rows_of(pair_ref, first, step), gain)
        mask = mask_ref[0, :, first * cols:(first + step) * cols]
        proj = dot(weight[:4 * chans], normed, 1, 1)
        terms = []
        for which, piece_refs in enumerate((left_refs, right_refs)):
            grad = load_chan(piece_refs, first, step) * mask
            value = proj[2 * which * chans:(2 * which + 1) * chans]
            gate = jax.nn.sigmoid(proj[(2 * which + 1) * chans:(2 * which + 2) * chans])
            through = grad * gate
            terms += [through.astype(BF16), (through * value * (1.0 - gate)).astype(BF16)]
        parts = [sigm_ref[first + t] for t in range(step)]
        terms.append(parts[0] if step == 1 else jnp.concatenate(parts, axis=1))
        g = dot(jnp.concatenate(terms, axis=0), weight, 0, 0) * gain
        grad_in = scaled * (
            g - jnp.mean(g, axis=1, keepdims=True) - hat * jnp.mean(g * hat, axis=1, keepdims=True)
        )
        out_ref[first:first + step] = grad_in.reshape(step, cols, chans).astype(BF16)


def gather_kernel(*refs):
    out_ref = refs[-1]
    cols = refs[0].shape[2]
    for s, ref in enumerate(refs[:-1]):
        out_ref[:, :, s * cols:(s + 1) * cols] = turn(ref[...]).astype(BF16)


def split_kernel(terms, *refs):
    in_refs, out_refs = refs[:terms], refs[terms:]
    cols = out_refs[0].shape[2]
    for s, ref in enumerate(out_refs):
        part = slice(s * cols, (s + 1) * cols)
        total = in_refs[0][:, :, part].astype(F32)
        for other in in_refs[1:]:
            total += other[:, :, part].astype(F32)
        ref[...] = turn(total.astype(BF16)).astype(BF16)


def block_of(right_refs, chunks, u, b, c, cols):
    parts = [ref[c] for ref in right_refs[u * chunks:(u + 1) * chunks]]
    rows = parts[0] if chunks == 1 else jnp.concatenate(parts, axis=0)
    return rows[b * cols:(b + 1) * cols]


def combine_kernel(groups, peers, chunks, place_ref, *refs):
    count = peers * chunks
    right_refs, left_refs, out_refs = refs[:count], refs[count:count + groups], refs[count + groups:-2]
    left_buf, sums = refs[-2:]
    rows, own, cols = left_refs[0].shape
    span = groups // peers
    for s, ref in enumerate(left_refs):
        left_buf[:, :, s * cols:(s + 1) * cols] = turn(ref[...]).astype(BF16)
    for n in range(groups):
        place = place_ref[n]
        for c in range(own):
            sums[place, c] = dot(left_buf[c], block_of(right_refs, chunks, n // span, n % span, c, cols), 1, 1)
    for s, ref in enumerate(out_refs):
        ref[...] = turn(sums[s]).astype(BF16)


def left_kernel(groups, peers, chunks, place_ref, *refs):
    count = peers * chunks
    right_refs, grad_refs, out_refs = refs[:count], refs[count:count + groups], refs[count + groups:-2]
    grads, sums = refs[-2:]
    rows, own, cols = grad_refs[0].shape
    span = groups // peers
    for s, ref in enumerate(grad_refs):
        grads[s] = turn(ref[...]).astype(BF16)
    for c in range(own):
        total = 0.0
        for n in range(groups):
            block = block_of(right_refs, chunks, n // span, n % span, c, cols)
            total += dot(grads[place_ref[n], c], block, 1, 0)
        sums[c] = total
    for s, ref in enumerate(out_refs):
        ref[...] = turn(sums[:, :, s * cols:(s + 1) * cols]).astype(BF16)


def right_kernel(groups, peers, chunks, place_ref, *refs):
    count = groups * chunks
    grad_refs, left_refs, out_refs = refs[:count], refs[count:2 * count], refs[2 * count:-2]
    grads, left_buf = refs[-2:]
    rows, own, cols = grad_refs[0].shape
    span = groups // peers
    for n, (grad_ref, left_ref) in enumerate(zip(grad_refs, left_refs)):
        piece, s = divmod(n, groups)
        part = slice(piece * rows, (piece + 1) * rows)
        grads[s, :, part] = turn(grad_ref[...]).astype(BF16)
        left_buf[:, part, s * cols:(s + 1) * cols] = turn(left_ref[...]).astype(BF16)
    for n in range(groups):
        place = place_ref[n]
        u, b = divmod(n, span)
        for c in range(own):
            total = dot(grads[place, c], left_buf[c], 0, 0).astype(BF16)
            for h in range(chunks):
                low, high = max(b * cols, h * rows), min((b + 1) * cols, (h + 1) * rows)
                if low < high:
                    out_refs[u * chunks + h][c, low - h * rows:high - h * rows] = total[
                        low - b * cols:high - b * cols
                    ]


def local(chunks, pair, grad_out, token_mask, ln_gain, proj_weights, gate_weight, out_weight, out_gain):
    rows, cols, chans = pair.shape
    groups = lax.axis_size("ch")
    sides, cores = lax.axis_size("row"), lax.axis_size("sub")
    row_blocks = sides * cores
    own = chans // groups
    tokens = rows * row_blocks
    part_rows = rows // chunks
    block = min(8, part_rows)
    blocks = part_rows // block
    step = 4 if cols % 128 == 0 and block % 4 == 0 else 1
    some = 16 if own % 16 == 0 else own
    z = lax.axis_index("ch")
    span = groups // row_blocks
    me = lax.axis_index(ROWS)
    place = jnp.stack([z ^ ((me ^ (n // span)) * span + n % span) for n in range(groups)]).astype(jnp.int32)

    def mine(array, axis):
        parts = [lax.dynamic_slice_in_dim(array, (z ^ s) * own, own, axis) for s in range(groups)]
        return jnp.concatenate(parts, axis=axis)

    mask_float = token_mask.astype(F32)
    row_mask = lax.dynamic_slice_in_dim(mask_float, lax.axis_index(ROWS) * rows, rows)
    col_mask = lax.dynamic_slice_in_dim(mask_float, z * cols, cols)
    mask = (row_mask[:, None] * col_mask[None, :]).reshape(rows // block, 1, block * cols)
    gain = ln_gain.reshape(1, chans)
    proj_t = mine(jnp.swapaxes(proj_weights, 1, 2), 1)
    left_w = proj_t[:2].reshape(2 * chans, chans)
    right_w = proj_t[2:].reshape(2 * chans, chans)
    gate_t = gate_weight.T
    all_w = jnp.concatenate([left_w, right_w, gate_t], axis=0)
    out_w = mine(out_weight, 0)
    out_t = out_w.T
    gain_col = mine(out_gain, 0).reshape(chans, 1)
    eye = jnp.eye(chans, dtype=BF16)

    params = pltpu.CompilerParams(vmem_limit_bytes=VMEM_LIMIT)

    def cost(flops, arrays):
        return pl.CostEstimate(
            flops=flops, bytes_accessed=arrays * part_rows * cols * chans * 2, transcendentals=0
        )

    pairs = part_rows * cols

    def row_spec(first):
        return pl.BlockSpec((block, cols, chans), lambda s: (first + s, 0, 0))

    def mask_spec(first):
        return pl.BlockSpec((1, 1, block * cols), lambda s: (first + s, 0, 0))

    def whole(array):
        return pl.BlockSpec(array.shape, lambda s: (0,) * array.ndim)

    piece_spec = pl.BlockSpec((block, own, cols), lambda s: (s, 0, 0))
    sigm_spec = pl.BlockSpec((block, chans, cols), lambda s: (s, 0, 0))

    def pieces(count):
        return [jax.ShapeDtypeStruct((count, own, cols), BF16)] * groups

    def project(weight, first, count):
        return pl.pallas_call(
            functools.partial(project_kernel, step),
            grid=(count,),
            in_specs=[row_spec(first), mask_spec(first), whole(gain), whole(weight)],
            out_specs=[piece_spec] * groups,
            out_shape=pieces(count * block),
            compiler_params=params,
            cost_estimate=cost(4 * chans * chans * count * block * cols, 2 * count // blocks),
        )(pair, mask, gain, weight)

    def middle(comb, first):
        return pl.pallas_call(
            functools.partial(middle_kernel, step, groups),
            grid=(blocks,),
            in_specs=[row_spec(first), row_spec(first), whole(gain), whole(gate_t), whole(out_w),
                      whole(out_t), whole(gain_col), whole(eye)] + [piece_spec] * groups,
            out_specs=[piece_spec] * groups + [sigm_spec],
            out_shape=pieces(part_rows) + [jax.ShapeDtypeStruct((part_rows, chans, cols), BF16)],
            compiler_params=params,
            cost_estimate=cost(8 * chans * chans * pairs, 5),
        )(pair, grad_out, gain, gate_t, out_w, out_t, gain_col, eye, *comb)

    def last(left_grad, right_grad, sigm, first, held):
        return pl.pallas_call(
            functools.partial(last_kernel, step, groups),
            grid=(blocks,),
            in_specs=[row_spec(first), sigm_spec, mask_spec(first), whole(gain), whole(all_w),
                      pl.BlockSpec(memory_space=pl.ANY)] + [piece_spec] * (2 * groups),
            out_specs=row_spec(first),
            out_shape=jax.ShapeDtypeStruct((rows, cols, chans), BF16),
            input_output_aliases={5: 0},
            compiler_params=params,
            cost_estimate=cost(18 * chans * chans * pairs, 5),
        )(pair, sigm, mask, gain, all_w, held, *left_grad, *right_grad)

    def exchange(sent):
        return [sent[0]] + [
            lax.ppermute(sent[s], "ch", [(a, a ^ s) for a in range(groups)]) for s in range(1, groups)
        ]

    def chan_spec(count):
        return pl.BlockSpec((count, some, cols), lambda g, *_: (0, g, 0))

    flat_spec = pl.BlockSpec((some, part_rows, tokens), lambda g, *_: (g, 0, 0))
    flat_shape = jax.ShapeDtypeStruct((own, part_rows, tokens), BF16)

    def gather(got):
        return pl.pallas_call(
            gather_kernel,
            grid=(own // some,),
            in_specs=[chan_spec(part_rows)] * groups,
            out_specs=flat_spec,
            out_shape=flat_shape,
            compiler_params=params,
            cost_estimate=cost(0, 2),
        )(*got)

    def split(terms):
        return pl.pallas_call(
            functools.partial(split_kernel, len(terms)),
            grid=(own // some,),
            in_specs=[flat_spec] * len(terms),
            out_specs=[chan_spec(part_rows)] * groups,
            out_shape=pieces(part_rows),
            compiler_params=params,
            cost_estimate=cost(0, 1 + len(terms)),
        )(*terms)

    def swap(array, axis, by):
        return lax.ppermute(array, axis, [(a, a ^ by) for a in range(lax.axis_size(axis))])

    def all_rows(array):
        blocks = []
        for x in range(sides):
            came = swap(array, "row", x) if x else array
            blocks += [swap(came, "sub", c) if c else came for c in range(cores)]
        return blocks

    def own_rows(partials):
        terms = []
        for x in range(sides):
            of_cores = [swap(partials[x * cores + c], "sub", c) if c else partials[x * cores] for c in range(cores)]
            if x:
                total = sum(term.astype(F32) for term in of_cores).astype(BF16)
                terms.append(swap(total, "row", x))
            else:
                terms += of_cores
        return terms

    product = 2 * part_rows * tokens * tokens * own

    def with_right(kernel, got, scratch):
        return pl.pallas_call(
            functools.partial(kernel, groups, row_blocks, chunks),
            grid_spec=pltpu.PrefetchScalarGridSpec(
                num_scalar_prefetch=1, grid=(own // some,),
                in_specs=[flat_spec] * (row_blocks * chunks) + [chan_spec(part_rows)] * groups,
                out_specs=[chan_spec(part_rows)] * groups,
                scratch_shapes=scratch,
            ),
            out_shape=pieces(part_rows),
            compiler_params=params,
            cost_estimate=cost(product, 2 + row_blocks * chunks),
        )(place, *right, *got)

    def combine(left):
        return with_right(combine_kernel, left, [
            pltpu.VMEM((some, part_rows, tokens), BF16), pltpu.VMEM((groups, some, part_rows, cols), F32)
        ])

    def left_back(grad):
        return with_right(left_kernel, grad, [
            pltpu.VMEM((groups, some, part_rows, cols), BF16), pltpu.VMEM((some, part_rows, tokens), F32)
        ])

    def right_back(grads, lefts):
        count = row_blocks * chunks
        out = pl.pallas_call(
            functools.partial(right_kernel, groups, row_blocks, chunks),
            grid_spec=pltpu.PrefetchScalarGridSpec(
                num_scalar_prefetch=1, grid=(own // some,),
                in_specs=[chan_spec(part_rows)] * (2 * groups * chunks),
                out_specs=[flat_spec] * count,
                scratch_shapes=[
                    pltpu.VMEM((groups, some, rows, cols), BF16), pltpu.VMEM((some, rows, tokens), BF16)
                ],
            ),
            out_shape=[flat_shape] * count,
            compiler_params=params,
            cost_estimate=cost(product * chunks, (2 + row_blocks) * chunks),
        )(place, *sum(grads, []), *sum(lefts, []))
        return [out[h::chunks] for h in range(chunks)]

    def tie(*lists):
        values = iter(lax.optimization_barrier(tuple(sum(lists, []))))
        return [[next(values) for _ in part] for part in lists]

    firsts = [p * blocks for p in range(chunks)]
    sent = [list(project(weight, first, blocks)) for weight in (right_w, left_w) for first in firsts]
    halves, gathered = [], []
    for part in range(chunks):
        got = exchange(sent[part])
        got = tie(got, gathered, *sent[part + 1:part + 1 + chunks])[0]
        gathered = [gather(got)]
        halves.append(all_rows(gathered[0]))
    right = [half[u] for u in range(row_blocks) for half in halves]
    lefts = [exchange(pieces_of) for pieces_of in sent[chunks:]]
    sigms, grads, backs = [], [], []
    for first, left in zip(firsts, lefts):
        *grad_comb, sigm = middle(exchange(combine(left)), first)
        sigms.append(sigm)
        grads.append(exchange(grad_comb))
    for part in range(chunks):
        backs.append(list(left_back(grads[part])))
        if part == 0 and chunks > 1:
            grads[-1] = tie(grads[-1], backs[0])[0]
    left_grads = [exchange(back) for back in backs]
    right_grads = [exchange(split(own_rows(partials))) for partials in right_back(grads, lefts)]
    out = jnp.zeros((rows, cols, chans), BF16)
    for first, left_grad, right_grad, sigm in zip(firsts, left_grads, right_grads, sigms):
        out = last(left_grad, right_grad, sigm, first, out)
    return out


def solution(mesh):
    spread = P(("rep", "row", "sub"), "ch", None)
    return jax.shard_map(
        functools.partial(local, 2),
        mesh=mesh,
        in_specs=(spread, spread, P("rep"), P(), P(), P(), P(), P()),
        out_specs=spread,
        check_vma=False,
    )
```

```python
import functools

import jax
import jax.numpy as jnp
from jax import lax
from jax.experimental import pallas as pl
from jax.experimental.pallas import tpu as pltpu
from jax.sharding import PartitionSpec as P

epsilon = 1e-05
F32 = jnp.float32
BF16 = jnp.bfloat16
VMEM_LIMIT = 56 * 1024 * 1024
ROWS = ("row", "sub")


def dot(a, b, ca, cb):
    return lax.dot_general(a, b, (((ca,), (cb,)), ((), ())), preferred_element_type=F32)


def turn(block):
    return jnp.swapaxes(block.astype(F32), 0, 1)


def norm_rows(pair_block, gain):
    x = pair_block.astype(F32)
    center = x - jnp.mean(x, axis=1, keepdims=True)
    scaled = lax.rsqrt(jnp.mean(center * center, axis=1, keepdims=True) + epsilon)
    hat = center * scaled
    return hat, scaled, (hat * gain).astype(BF16)


def rows_of(ref, first, count):
    block = ref[first:first + count]
    return block.reshape(count * block.shape[1], block.shape[2])


def load_chan(refs, first, count):
    parts = [jnp.concatenate([ref[first + t].astype(F32) for ref in refs], axis=0) for t in range(count)]
    return parts[0] if count == 1 else jnp.concatenate(parts, axis=1)


def store_chan(refs, first, count, value):
    _, own, cols = refs[0].shape
    for s, ref in enumerate(refs):
        group = value[s * own:(s + 1) * own].astype(BF16)
        for t in range(count):
            ref[first + t] = group[:, t * cols:(t + 1) * cols] if count > 1 else group


def project_kernel(step, pair_ref, mask_ref, gain_ref, weight_ref, *out_refs):
    rows, cols, chans = pair_ref.shape
    for first in range(0, rows, step):
        _, _, normed = norm_rows(rows_of(pair_ref, first, step), gain_ref[...])
        both = dot(weight_ref[...], normed, 1, 1)
        mask = mask_ref[0, :, first * cols:(first + step) * cols]
        store_chan(out_refs, first, step, mask * jax.nn.sigmoid(both[chans:]) * both[:chans])


def middle_kernel(
    step, groups, pair_ref, gout_ref, gain_ref, gate_t_ref, out_w_ref, out_t_ref, out_gain_ref, eye_ref, *refs
):
    comb_refs, gcomb_refs, sigm_ref = refs[:groups], refs[groups:2 * groups], refs[2 * groups]
    rows, cols, chans = pair_ref.shape
    out_gain = out_gain_ref[...]
    for first in range(0, rows, step):
        _, _, normed = norm_rows(rows_of(pair_ref, first, step), gain_ref[...])
        gate = jax.nn.sigmoid(dot(gate_t_ref[...], normed, 1, 1))
        gout = dot(eye_ref[...], rows_of(gout_ref, first, step), 1, 1)
        comb = load_chan(comb_refs, first, step)
        center = comb - jnp.mean(comb, axis=0, keepdims=True)
        scaled = lax.rsqrt(jnp.mean(center * center, axis=0, keepdims=True) + epsilon)
        hat = center * scaled
        lin = dot(out_t_ref[...], (hat * out_gain).astype(BF16), 1, 0)
        grad_lin = (gout * gate).astype(BF16)
        h = dot(out_w_ref[...], grad_lin, 1, 0) * out_gain
        grad = scaled * (
            h - jnp.mean(h, axis=0, keepdims=True) - hat * jnp.mean(h * hat, axis=0, keepdims=True)
        )
        store_chan(gcomb_refs, first, step, grad)
        sigm = (gout * lin * gate * (1.0 - gate)).astype(BF16)
        for t in range(step):
            sigm_ref[first + t] = sigm[:, t * cols:(t + 1) * cols] if step > 1 else sigm


def last_kernel(step, groups, pair_ref, sigm_ref, mask_ref, gain_ref, weight_ref, held_ref, *refs):
    del held_ref
    left_refs, right_refs, out_ref = refs[:groups], refs[groups:2 * groups], refs[2 * groups]
    rows, cols, chans = pair_ref.shape
    gain = gain_ref[...]
    weight = weight_ref[...]
    for first in range(0, rows, step):
        hat, scaled, normed = norm_rows(rows_of(pair_ref, first, step), gain)
        mask = mask_ref[0, :, first * cols:(first + step) * cols]
        proj = dot(weight[:4 * chans], normed, 1, 1)
        terms = []
        for which, piece_refs in enumerate((left_refs, right_refs)):
            grad = load_chan(piece_refs, first, step) * mask
            value = proj[2 * which * chans:(2 * which + 1) * chans]
            gate = jax.nn.sigmoid(proj[(2 * which + 1) * chans:(2 * which + 2) * chans])
            through = grad * gate
            terms += [through.astype(BF16), (through * value * (1.0 - gate)).astype(BF16)]
        parts = [sigm_ref[first + t] for t in range(step)]
        terms.append(parts[0] if step == 1 else jnp.concatenate(parts, axis=1))
        g = dot(jnp.concatenate(terms, axis=0), weight, 0, 0) * gain
        grad_in = scaled * (
            g - jnp.mean(g, axis=1, keepdims=True) - hat * jnp.mean(g * hat, axis=1, keepdims=True)
        )
        out_ref[first:first + step] = grad_in.reshape(step, cols, chans).astype(BF16)


def gather_kernel(*refs):
    out_ref = refs[-1]
    cols = refs[0].shape[2]
    for s, ref in enumerate(refs[:-1]):
        out_ref[:, :, s * cols:(s + 1) * cols] = turn(ref[...]).astype(BF16)


def split_kernel(terms, *refs):
    in_refs, out_refs = refs[:terms], refs[terms:]
    cols = out_refs[0].shape[2]
    for s, ref in enumerate(out_refs):
        part = slice(s * cols, (s + 1) * cols)
        total = in_refs[0][:, :, part].astype(F32)
        for other in in_refs[1:]:
            total += other[:, :, part].astype(F32)
        ref[...] = turn(total.astype(BF16)).astype(BF16)


def block_of(right_refs, chunks, u, b, c, cols):
    parts = [ref[c] for ref in right_refs[u * chunks:(u + 1) * chunks]]
    rows = parts[0] if chunks == 1 else jnp.concatenate(parts, axis=0)
    return rows[b * cols:(b + 1) * cols]


def combine_kernel(groups, peers, chunks, place_ref, *refs):
    count = peers * chunks
    right_refs, left_refs, out_refs = refs[:count], refs[count:count + groups], refs[count + groups:-2]
    left_buf, sums = refs[-2:]
    rows, own, cols = left_refs[0].shape
    span = groups // peers
    for s, ref in enumerate(left_refs):
        left_buf[:, :, s * cols:(s + 1) * cols] = turn(ref[...]).astype(BF16)
    for n in range(groups):
        place = place_ref[n]
        for c in range(own):
            sums[place, c] = dot(left_buf[c], block_of(right_refs, chunks, n // span, n % span, c, cols), 1, 1)
    for s, ref in enumerate(out_refs):
        ref[...] = turn(sums[s]).astype(BF16)


def left_kernel(groups, peers, chunks, place_ref, *refs):
    count = peers * chunks
    right_refs, grad_refs, out_refs = refs[:count], refs[count:count + groups], refs[count + groups:-2]
    grads, sums = refs[-2:]
    rows, own, cols = grad_refs[0].shape
    span = groups // peers
    for s, ref in enumerate(grad_refs):
        grads[s] = turn(ref[...]).astype(BF16)
    for c in range(own):
        total = 0.0
        for n in range(groups):
            block = block_of(right_refs, chunks, n // span, n % span, c, cols)
            total += dot(grads[place_ref[n], c], block, 1, 0)
        sums[c] = total
    for s, ref in enumerate(out_refs):
        ref[...] = turn(sums[:, :, s * cols:(s + 1) * cols]).astype(BF16)


def right_kernel(groups, peers, chunks, place_ref, *refs):
    count = groups * chunks
    grad_refs, left_refs, out_refs = refs[:count], refs[count:2 * count], refs[2 * count:-2]
    grads, left_buf = refs[-2:]
    rows, own, cols = grad_refs[0].shape
    span = groups // peers
    for n, (grad_ref, left_ref) in enumerate(zip(grad_refs, left_refs)):
        piece, s = divmod(n, groups)
        part = slice(piece * rows, (piece + 1) * rows)
        grads[s, :, part] = turn(grad_ref[...]).astype(BF16)
        left_buf[:, part, s * cols:(s + 1) * cols] = turn(left_ref[...]).astype(BF16)
    for n in range(groups):
        place = place_ref[n]
        u, b = divmod(n, span)
        for c in range(own):
            total = dot(grads[place, c], left_buf[c], 0, 0).astype(BF16)
            for h in range(chunks):
                low, high = max(b * cols, h * rows), min((b + 1) * cols, (h + 1) * rows)
                if low < high:
                    out_refs[u * chunks + h][c, low - h * rows:high - h * rows] = total[
                        low - b * cols:high - b * cols
                    ]


def local(chunks, pair, grad_out, token_mask, ln_gain, proj_weights, gate_weight, out_weight, out_gain):
    rows, cols, chans = pair.shape
    groups = lax.axis_size("ch")
    sides, cores = lax.axis_size("row"), lax.axis_size("sub")
    row_blocks = sides * cores
    own = chans // groups
    tokens = rows * row_blocks
    part_rows = rows // chunks
    block = min(8, part_rows)
    blocks = part_rows // block
    step = 4 if cols % 128 == 0 and block % 4 == 0 else 1
    some = 16 if own % 16 == 0 else own
    z = lax.axis_index("ch")
    span = groups // row_blocks
    me = lax.axis_index(ROWS)
    place = jnp.stack([z ^ ((me ^ (n // span)) * span + n % span) for n in range(groups)]).astype(jnp.int32)

    def mine(array, axis):
        parts = [lax.dynamic_slice_in_dim(array, (z ^ s) * own, own, axis) for s in range(groups)]
        return jnp.concatenate(parts, axis=axis)

    mask_float = token_mask.astype(F32)
    row_mask = lax.dynamic_slice_in_dim(mask_float, lax.axis_index(ROWS) * rows, rows)
    col_mask = lax.dynamic_slice_in_dim(mask_float, z * cols, cols)
    mask = (row_mask[:, None] * col_mask[None, :]).reshape(rows // block, 1, block * cols)
    gain = ln_gain.reshape(1, chans)
    proj_t = mine(jnp.swapaxes(proj_weights, 1, 2), 1)
    left_w = proj_t[:2].reshape(2 * chans, chans)
    right_w = proj_t[2:].reshape(2 * chans, chans)
    gate_t = gate_weight.T
    all_w = jnp.concatenate([left_w, right_w, gate_t], axis=0)
    out_w = mine(out_weight, 0)
    out_t = out_w.T
    gain_col = mine(out_gain, 0).reshape(chans, 1)
    eye = jnp.eye(chans, dtype=BF16)

    params = pltpu.CompilerParams(vmem_limit_bytes=VMEM_LIMIT)

    def cost(flops, arrays):
        return pl.CostEstimate(
            flops=flops, bytes_accessed=arrays * part_rows * cols * chans * 2, transcendentals=0
        )

    pairs = part_rows * cols

    def row_spec(first):
        return pl.BlockSpec((block, cols, chans), lambda s: (first + s, 0, 0))

    def mask_spec(first):
        return pl.BlockSpec((1, 1, block * cols), lambda s: (first + s, 0, 0))

    def whole(array):
        return pl.BlockSpec(array.shape, lambda s: (0,) * array.ndim)

    piece_spec = pl.BlockSpec((block, own, cols), lambda s: (s, 0, 0))
    sigm_spec = pl.BlockSpec((block, chans, cols), lambda s: (s, 0, 0))

    def pieces(count):
        return [jax.ShapeDtypeStruct((count, own, cols), BF16)] * groups

    def project(weight, first, count):
        return pl.pallas_call(
            functools.partial(project_kernel, step),
            grid=(count,),
            in_specs=[row_spec(first), mask_spec(first), whole(gain), whole(weight)],
            out_specs=[piece_spec] * groups,
            out_shape=pieces(count * block),
            compiler_params=params,
            cost_estimate=cost(4 * chans * chans * count * block * cols, 2 * count // blocks),
        )(pair, mask, gain, weight)

    def middle(comb, first):
        return pl.pallas_call(
            functools.partial(middle_kernel, step, groups),
            grid=(blocks,),
            in_specs=[row_spec(first), row_spec(first), whole(gain), whole(gate_t), whole(out_w),
                      whole(out_t), whole(gain_col), whole(eye)] + [piece_spec] * groups,
            out_specs=[piece_spec] * groups + [sigm_spec],
            out_shape=pieces(part_rows) + [jax.ShapeDtypeStruct((part_rows, chans, cols), BF16)],
            compiler_params=params,
            cost_estimate=cost(8 * chans * chans * pairs, 5),
        )(pair, grad_out, gain, gate_t, out_w, out_t, gain_col, eye, *comb)

    def last(left_grad, right_grad, sigm, first, held):
        return pl.pallas_call(
            functools.partial(last_kernel, step, groups),
            grid=(blocks,),
            in_specs=[row_spec(first), sigm_spec, mask_spec(first), whole(gain), whole(all_w),
                      pl.BlockSpec(memory_space=pl.ANY)] + [piece_spec] * (2 * groups),
            out_specs=row_spec(first),
            out_shape=jax.ShapeDtypeStruct((rows, cols, chans), BF16),
            input_output_aliases={5: 0},
            compiler_params=params,
            cost_estimate=cost(18 * chans * chans * pairs, 5),
        )(pair, sigm, mask, gain, all_w, held, *left_grad, *right_grad)

    def exchange(sent):
        return [sent[0]] + [
            lax.ppermute(sent[s], "ch", [(a, a ^ s) for a in range(groups)]) for s in range(1, groups)
        ]

    def chan_spec(count):
        return pl.BlockSpec((count, some, cols), lambda g, *_: (0, g, 0))

    flat_spec = pl.BlockSpec((some, part_rows, tokens), lambda g, *_: (g, 0, 0))
    flat_shape = jax.ShapeDtypeStruct((own, part_rows, tokens), BF16)

    def gather(got):
        return pl.pallas_call(
            gather_kernel,
            grid=(own // some,),
            in_specs=[chan_spec(part_rows)] * groups,
            out_specs=flat_spec,
            out_shape=flat_shape,
            compiler_params=params,
            cost_estimate=cost(0, 2),
        )(*got)

    def split(terms):
        return pl.pallas_call(
            functools.partial(split_kernel, len(terms)),
            grid=(own // some,),
            in_specs=[flat_spec] * len(terms),
            out_specs=[chan_spec(part_rows)] * groups,
            out_shape=pieces(part_rows),
            compiler_params=params,
            cost_estimate=cost(0, 1 + len(terms)),
        )(*terms)

    def tie(*lists):
        values = iter(lax.optimization_barrier(tuple(sum(lists, []))))
        return [[next(values) for _ in part] for part in lists]

    def swap(array, axis, by):
        return lax.ppermute(array, axis, [(a, a ^ by) for a in range(lax.axis_size(axis))])

    def all_rows(array, sent):
        blocks, moved = [], []
        for x in range(sides):
            came = swap(sent, "row", x) if x else array
            moved += [came] if x else []
            blocks += [swap(came, "sub", c) if c else came for c in range(cores)]
        return blocks, moved

    def own_rows(partials, before):
        terms = []
        for x in range(sides):
            of_cores = [swap(partials[x * cores + c], "sub", c) if c else partials[x * cores] for c in range(cores)]
            if x:
                total = sum(term.astype(F32) for term in of_cores).astype(BF16)
                terms.append(swap(tie([total], before)[0][0], "row", x))
            else:
                terms += of_cores
        return terms

    product = 2 * part_rows * tokens * tokens * own

    def with_right(kernel, got, scratch):
        return pl.pallas_call(
            functools.partial(kernel, groups, row_blocks, chunks),
            grid_spec=pltpu.PrefetchScalarGridSpec(
                num_scalar_prefetch=1, grid=(own // some,),
                in_specs=[flat_spec] * (row_blocks * chunks) + [chan_spec(part_rows)] * groups,
                out_specs=[chan_spec(part_rows)] * groups,
                scratch_shapes=scratch,
            ),
            out_shape=pieces(part_rows),
            compiler_params=params,
            cost_estimate=cost(product, 2 + row_blocks * chunks),
        )(place, *right, *got)

    def combine(left):
        return with_right(combine_kernel, left, [
            pltpu.VMEM((some, part_rows, tokens), BF16), pltpu.VMEM((groups, some, part_rows, cols), F32)
        ])

    def left_back(grad):
        return with_right(left_kernel, grad, [
            pltpu.VMEM((groups, some, part_rows, cols), BF16), pltpu.VMEM((some, part_rows, tokens), F32)
        ])

    def right_back(grads, lefts):
        count = row_blocks * chunks
        out = pl.pallas_call(
            functools.partial(right_kernel, groups, row_blocks, chunks),
            grid_spec=pltpu.PrefetchScalarGridSpec(
                num_scalar_prefetch=1, grid=(own // some,),
                in_specs=[chan_spec(part_rows)] * (2 * groups * chunks),
                out_specs=[flat_spec] * count,
                scratch_shapes=[
                    pltpu.VMEM((groups, some, rows, cols), BF16), pltpu.VMEM((some, rows, tokens), BF16)
                ],
            ),
            out_shape=[flat_shape] * count,
            compiler_params=params,
            cost_estimate=cost(product * chunks, (2 + row_blocks) * chunks),
        )(place, *sum(grads, []), *sum(lefts, []))
        return [out[h::chunks] for h in range(chunks)]

    firsts = [p * blocks for p in range(chunks)]
    sent = [list(project(weight, first, blocks)) for weight in (right_w, left_w) for first in firsts]
    lefts = [exchange(pieces_of) for pieces_of in sent[chunks:]]
    halves, moved = [], []
    for part in range(chunks):
        got = tie(exchange(sent[part]), moved, *sent[part + 1:part + 1 + chunks])[0]
        block_here = gather(got)
        over = tie([block_here], lefts[part - 1][1:3])[0][0] if part else block_here
        row_parts, moved = all_rows(block_here, over)
        halves.append(row_parts)
    right = [half[u] for u in range(row_blocks) for half in halves]
    sigms, grads, backs = [], [], []
    for first, left in zip(firsts, lefts):
        *grad_comb, sigm = middle(exchange(combine(left)), first)
        sigms.append(sigm)
        grads.append(exchange(grad_comb))
    for part in range(chunks):
        backs.append(list(left_back(grads[part])))
        if part == 0 and chunks > 1:
            grads[-1] = tie(grads[-1], backs[0])[0]
    left_grads = [exchange(back) for back in backs]
    right_grads = [
        exchange(split(own_rows(partials, back[1:3]))) for partials, back in zip(right_back(grads, lefts), left_grads)
    ]
    out = jnp.zeros((rows, cols, chans), BF16)
    for first, left_grad, right_grad, sigm in zip(firsts, left_grads, right_grads, sigms):
        out = last(left_grad, right_grad, sigm, first, out)
    return out


def solution(mesh):
    spread = P(("rep", "row", "sub"), "ch", None)
    return jax.shard_map(
        functools.partial(local, 2),
        mesh=mesh,
        in_specs=(spread, spread, P("rep"), P(), P(), P(), P(), P()),
        out_specs=spread,
        check_vma=False,
    )
```

```python
import functools

import jax
import jax.numpy as jnp
from jax import lax
from jax.experimental import pallas as pl
from jax.experimental.pallas import tpu as pltpu
from jax.sharding import PartitionSpec as P

epsilon = 1e-05
F32 = jnp.float32
BF16 = jnp.bfloat16
VMEM_LIMIT = 56 * 1024 * 1024
ROWS = ("row", "sub")


def dot(a, b, ca, cb):
    return lax.dot_general(a, b, (((ca,), (cb,)), ((), ())), preferred_element_type=F32)


def turn(block):
    return jnp.swapaxes(block.astype(F32), 0, 1)


def norm_rows(pair_block, gain):
    x = pair_block.astype(F32)
    center = x - jnp.mean(x, axis=1, keepdims=True)
    scaled = lax.rsqrt(jnp.mean(center * center, axis=1, keepdims=True) + epsilon)
    hat = center * scaled
    return hat, scaled, (hat * gain).astype(BF16)


def rows_of(ref, first, count):
    block = ref[first:first + count]
    return block.reshape(count * block.shape[1], block.shape[2])


def load_chan(refs, first, count):
    parts = [jnp.concatenate([ref[first + t].astype(F32) for ref in refs], axis=0) for t in range(count)]
    return parts[0] if count == 1 else jnp.concatenate(parts, axis=1)


def store_chan(refs, first, count, value):
    _, own, cols = refs[0].shape
    for s, ref in enumerate(refs):
        group = value[s * own:(s + 1) * own].astype(BF16)
        for t in range(count):
            ref[first + t] = group[:, t * cols:(t + 1) * cols] if count > 1 else group


def project_kernel(step, pair_ref, mask_ref, gain_ref, weight_ref, *out_refs):
    rows, cols, chans = pair_ref.shape
    for first in range(0, rows, step):
        _, _, normed = norm_rows(rows_of(pair_ref, first, step), gain_ref[...])
        both = dot(weight_ref[...], normed, 1, 1)
        mask = mask_ref[0, :, first * cols:(first + step) * cols]
        store_chan(out_refs, first, step, mask * jax.nn.sigmoid(both[chans:]) * both[:chans])


def middle_kernel(
    step, groups, pair_ref, gout_ref, gain_ref, gate_t_ref, out_w_ref, out_t_ref, out_gain_ref, eye_ref, *refs
):
    comb_refs, gcomb_refs, sigm_ref = refs[:groups], refs[groups:2 * groups], refs[2 * groups]
    rows, cols, chans = pair_ref.shape
    out_gain = out_gain_ref[...]
    for first in range(0, rows, step):
        _, _, normed = norm_rows(rows_of(pair_ref, first, step), gain_ref[...])
        gate = jax.nn.sigmoid(dot(gate_t_ref[...], normed, 1, 1))
        gout = dot(eye_ref[...], rows_of(gout_ref, first, step), 1, 1)
        comb = load_chan(comb_refs, first, step)
        center = comb - jnp.mean(comb, axis=0, keepdims=True)
        scaled = lax.rsqrt(jnp.mean(center * center, axis=0, keepdims=True) + epsilon)
        hat = center * scaled
        lin = dot(out_t_ref[...], (hat * out_gain).astype(BF16), 1, 0)
        grad_lin = (gout * gate).astype(BF16)
        h = dot(out_w_ref[...], grad_lin, 1, 0) * out_gain
        grad = scaled * (
            h - jnp.mean(h, axis=0, keepdims=True) - hat * jnp.mean(h * hat, axis=0, keepdims=True)
        )
        store_chan(gcomb_refs, first, step, grad)
        sigm = (gout * lin * gate * (1.0 - gate)).astype(BF16)
        for t in range(step):
            sigm_ref[first + t] = sigm[:, t * cols:(t + 1) * cols] if step > 1 else sigm


def last_kernel(step, groups, pair_ref, sigm_ref, mask_ref, gain_ref, weight_ref, held_ref, *refs):
    del held_ref
    left_refs, right_refs, out_ref = refs[:groups], refs[groups:2 * groups], refs[2 * groups]
    rows, cols, chans = pair_ref.shape
    gain = gain_ref[...]
    weight = weight_ref[...]
    for first in range(0, rows, step):
        hat, scaled, normed = norm_rows(rows_of(pair_ref, first, step), gain)
        mask = mask_ref[0, :, first * cols:(first + step) * cols]
        proj = dot(weight[:4 * chans], normed, 1, 1)
        terms = []
        for which, piece_refs in enumerate((left_refs, right_refs)):
            grad = load_chan(piece_refs, first, step) * mask
            value = proj[2 * which * chans:(2 * which + 1) * chans]
            gate = jax.nn.sigmoid(proj[(2 * which + 1) * chans:(2 * which + 2) * chans])
            through = grad * gate
            terms += [through.astype(BF16), (through * value * (1.0 - gate)).astype(BF16)]
        parts = [sigm_ref[first + t] for t in range(step)]
        terms.append(parts[0] if step == 1 else jnp.concatenate(parts, axis=1))
        g = dot(jnp.concatenate(terms, axis=0), weight, 0, 0) * gain
        grad_in = scaled * (
            g - jnp.mean(g, axis=1, keepdims=True) - hat * jnp.mean(g * hat, axis=1, keepdims=True)
        )
        out_ref[first:first + step] = grad_in.reshape(step, cols, chans).astype(BF16)


def gather_kernel(*refs):
    out_ref = refs[-1]
    cols = refs[0].shape[2]
    for s, ref in enumerate(refs[:-1]):
        out_ref[:, :, s * cols:(s + 1) * cols] = turn(ref[...]).astype(BF16)


def split_kernel(terms, *refs):
    in_refs, out_refs = refs[:terms], refs[terms:]
    cols = out_refs[0].shape[2]
    for s, ref in enumerate(out_refs):
        part = slice(s * cols, (s + 1) * cols)
        total = in_refs[0][:, :, part].astype(F32)
        for other in in_refs[1:]:
            total += other[:, :, part].astype(F32)
        ref[...] = turn(total.astype(BF16)).astype(BF16)


def block_of(right_refs, chunks, u, b, c, cols):
    parts = [ref[c] for ref in right_refs[u * chunks:(u + 1) * chunks]]
    rows = parts[0] if chunks == 1 else jnp.concatenate(parts, axis=0)
    return rows[b * cols:(b + 1) * cols]


def combine_kernel(groups, peers, chunks, place_ref, *refs):
    count = peers * chunks
    right_refs, left_refs, out_refs = refs[:count], refs[count:count + groups], refs[count + groups:-2]
    left_buf, sums = refs[-2:]
    rows, own, cols = left_refs[0].shape
    span = groups // peers
    for s, ref in enumerate(left_refs):
        left_buf[:, :, s * cols:(s + 1) * cols] = turn(ref[...]).astype(BF16)
    for n in range(groups):
        place = place_ref[n]
        for c in range(own):
            sums[place, c] = dot(left_buf[c], block_of(right_refs, chunks, n // span, n % span, c, cols), 1, 1)
    for s, ref in enumerate(out_refs):
        ref[...] = turn(sums[s]).astype(BF16)


def left_kernel(groups, peers, chunks, place_ref, *refs):
    count = peers * chunks
    right_refs, grad_refs, out_refs = refs[:count], refs[count:count + groups], refs[count + groups:-2]
    grads, sums = refs[-2:]
    rows, own, cols = grad_refs[0].shape
    span = groups // peers
    for s, ref in enumerate(grad_refs):
        grads[s] = turn(ref[...]).astype(BF16)
    for c in range(own):
        total = 0.0
        for n in range(groups):
            block = block_of(right_refs, chunks, n // span, n % span, c, cols)
            total += dot(grads[place_ref[n], c], block, 1, 0)
        sums[c] = total
    for s, ref in enumerate(out_refs):
        ref[...] = turn(sums[:, :, s * cols:(s + 1) * cols]).astype(BF16)


def right_kernel(groups, peers, chunks, place_ref, *refs):
    count = groups * chunks
    grad_refs, left_refs, out_refs = refs[:count], refs[count:2 * count], refs[2 * count:-2]
    grads, left_buf = refs[-2:]
    rows, own, cols = grad_refs[0].shape
    span = groups // peers
    for n, (grad_ref, left_ref) in enumerate(zip(grad_refs, left_refs)):
        piece, s = divmod(n, groups)
        part = slice(piece * rows, (piece + 1) * rows)
        grads[s, :, part] = turn(grad_ref[...]).astype(BF16)
        left_buf[:, part, s * cols:(s + 1) * cols] = turn(left_ref[...]).astype(BF16)
    for n in range(groups):
        place = place_ref[n]
        u, b = divmod(n, span)
        for c in range(own):
            total = dot(grads[place, c], left_buf[c], 0, 0).astype(BF16)
            for h in range(chunks):
                low, high = max(b * cols, h * rows), min((b + 1) * cols, (h + 1) * rows)
                if low < high:
                    out_refs[u * chunks + h][c, low - h * rows:high - h * rows] = total[
                        low - b * cols:high - b * cols
                    ]


def local(chunks, pair, grad_out, token_mask, ln_gain, proj_weights, gate_weight, out_weight, out_gain):
    rows, cols, chans = pair.shape
    groups = lax.axis_size("ch")
    sides, cores = lax.axis_size("row"), lax.axis_size("sub")
    row_blocks = sides * cores
    own = chans // groups
    tokens = rows * row_blocks
    part_rows = rows // chunks
    block = min(8, part_rows)
    blocks = part_rows // block
    step = 4 if cols % 128 == 0 and block % 4 == 0 else 1
    some = 16 if own % 16 == 0 else own
    z = lax.axis_index("ch")
    span = groups // row_blocks
    me = lax.axis_index(ROWS)
    place = jnp.stack([z ^ ((me ^ (n // span)) * span + n % span) for n in range(groups)]).astype(jnp.int32)

    def mine(array, axis):
        parts = [lax.dynamic_slice_in_dim(array, (z ^ s) * own, own, axis) for s in range(groups)]
        return jnp.concatenate(parts, axis=axis)

    mask_float = token_mask.astype(F32)
    row_mask = lax.dynamic_slice_in_dim(mask_float, lax.axis_index(ROWS) * rows, rows)
    col_mask = lax.dynamic_slice_in_dim(mask_float, z * cols, cols)
    mask = (row_mask[:, None] * col_mask[None, :]).reshape(rows // block, 1, block * cols)
    gain = ln_gain.reshape(1, chans)
    proj_t = mine(jnp.swapaxes(proj_weights, 1, 2), 1)
    left_w = proj_t[:2].reshape(2 * chans, chans)
    right_w = proj_t[2:].reshape(2 * chans, chans)
    gate_t = gate_weight.T
    all_w = jnp.concatenate([left_w, right_w, gate_t], axis=0)
    out_w = mine(out_weight, 0)
    out_t = out_w.T
    gain_col = mine(out_gain, 0).reshape(chans, 1)
    eye = jnp.eye(chans, dtype=BF16)

    params = pltpu.CompilerParams(vmem_limit_bytes=VMEM_LIMIT)

    def cost(flops, arrays):
        return pl.CostEstimate(
            flops=flops, bytes_accessed=arrays * part_rows * cols * chans * 2, transcendentals=0
        )

    pairs = part_rows * cols

    def row_spec(first):
        return pl.BlockSpec((block, cols, chans), lambda s: (first + s, 0, 0))

    def mask_spec(first):
        return pl.BlockSpec((1, 1, block * cols), lambda s: (first + s, 0, 0))

    def whole(array):
        return pl.BlockSpec(array.shape, lambda s: (0,) * array.ndim)

    piece_spec = pl.BlockSpec((block, own, cols), lambda s: (s, 0, 0))
    sigm_spec = pl.BlockSpec((block, chans, cols), lambda s: (s, 0, 0))

    def pieces(count):
        return [jax.ShapeDtypeStruct((count, own, cols), BF16)] * groups

    def project(weight, first, count):
        return pl.pallas_call(
            functools.partial(project_kernel, step),
            grid=(count,),
            in_specs=[row_spec(first), mask_spec(first), whole(gain), whole(weight)],
            out_specs=[piece_spec] * groups,
            out_shape=pieces(count * block),
            compiler_params=params,
            cost_estimate=cost(4 * chans * chans * count * block * cols, 2 * count // blocks),
        )(pair, mask, gain, weight)

    def middle(comb, first):
        return pl.pallas_call(
            functools.partial(middle_kernel, step, groups),
            grid=(blocks,),
            in_specs=[row_spec(first), row_spec(first), whole(gain), whole(gate_t), whole(out_w),
                      whole(out_t), whole(gain_col), whole(eye)] + [piece_spec] * groups,
            out_specs=[piece_spec] * groups + [sigm_spec],
            out_shape=pieces(part_rows) + [jax.ShapeDtypeStruct((part_rows, chans, cols), BF16)],
            compiler_params=params,
            cost_estimate=cost(8 * chans * chans * pairs, 5),
        )(pair, grad_out, gain, gate_t, out_w, out_t, gain_col, eye, *comb)

    def last(left_grad, right_grad, sigm, first, held):
        return pl.pallas_call(
            functools.partial(last_kernel, step, groups),
            grid=(blocks,),
            in_specs=[row_spec(first), sigm_spec, mask_spec(first), whole(gain), whole(all_w),
                      pl.BlockSpec(memory_space=pl.ANY)] + [piece_spec] * (2 * groups),
            out_specs=row_spec(first),
            out_shape=jax.ShapeDtypeStruct((rows, cols, chans), BF16),
            input_output_aliases={5: 0},
            compiler_params=params,
            cost_estimate=cost(18 * chans * chans * pairs, 5),
        )(pair, sigm, mask, gain, all_w, held, *left_grad, *right_grad)

    def exchange(sent):
        return [sent[0]] + [
            lax.ppermute(sent[s], "ch", [(a, a ^ s) for a in range(groups)]) for s in range(1, groups)
        ]

    def chan_spec(count):
        return pl.BlockSpec((count, some, cols), lambda g, *_: (0, g, 0))

    flat_spec = pl.BlockSpec((some, part_rows, tokens), lambda g, *_: (g, 0, 0))
    flat_shape = jax.ShapeDtypeStruct((own, part_rows, tokens), BF16)

    def gather(got):
        return pl.pallas_call(
            gather_kernel,
            grid=(own // some,),
            in_specs=[chan_spec(part_rows)] * groups,
            out_specs=flat_spec,
            out_shape=flat_shape,
            compiler_params=params,
            cost_estimate=cost(0, 2),
        )(*got)

    def split(terms):
        return pl.pallas_call(
            functools.partial(split_kernel, len(terms)),
            grid=(own // some,),
            in_specs=[flat_spec] * len(terms),
            out_specs=[chan_spec(part_rows)] * groups,
            out_shape=pieces(part_rows),
            compiler_params=params,
            cost_estimate=cost(0, 1 + len(terms)),
        )(*terms)

    def tie(*lists):
        values = iter(lax.optimization_barrier(tuple(sum(lists, []))))
        return [[next(values) for _ in part] for part in lists]

    def swap(array, axis, by):
        return lax.ppermute(array, axis, [(a, a ^ by) for a in range(lax.axis_size(axis))])

    def all_rows(array, before, beside):
        blocks = [swap(array, "sub", c) if c else array for c in range(cores)]
        sent = tie([array], blocks[1:], before)[0][0]
        for x in range(1, sides):
            came = tie([swap(sent, "row", x)], beside)[0][0]
            blocks += [swap(came, "sub", c) if c else came for c in range(cores)]
        return blocks

    def own_rows(partials, before):
        terms = []
        for x in range(sides):
            of_cores = [swap(partials[x * cores + c], "sub", c) if c else partials[x * cores] for c in range(cores)]
            if x:
                total = sum(term.astype(F32) for term in of_cores).astype(BF16)
                terms.append(swap(tie([total], before)[0][0], "row", x))
            else:
                terms += of_cores
        return terms

    product = 2 * part_rows * tokens * tokens * own

    def with_right(kernel, got, scratch):
        return pl.pallas_call(
            functools.partial(kernel, groups, row_blocks, chunks),
            grid_spec=pltpu.PrefetchScalarGridSpec(
                num_scalar_prefetch=1, grid=(own // some,),
                in_specs=[flat_spec] * (row_blocks * chunks) + [chan_spec(part_rows)] * groups,
                out_specs=[chan_spec(part_rows)] * groups,
                scratch_shapes=scratch,
            ),
            out_shape=pieces(part_rows),
            compiler_params=params,
            cost_estimate=cost(product, 2 + row_blocks * chunks),
        )(place, *right, *got)

    def combine(left):
        return with_right(combine_kernel, left, [
            pltpu.VMEM((some, part_rows, tokens), BF16), pltpu.VMEM((groups, some, part_rows, cols), F32)
        ])

    def left_back(grad):
        return with_right(left_kernel, grad, [
            pltpu.VMEM((groups, some, part_rows, cols), BF16), pltpu.VMEM((some, part_rows, tokens), F32)
        ])

    def right_back(grads, lefts):
        count = row_blocks * chunks
        out = pl.pallas_call(
            functools.partial(right_kernel, groups, row_blocks, chunks),
            grid_spec=pltpu.PrefetchScalarGridSpec(
                num_scalar_prefetch=1, grid=(own // some,),
                in_specs=[chan_spec(part_rows)] * (2 * groups * chunks),
                out_specs=[flat_spec] * count,
                scratch_shapes=[
                    pltpu.VMEM((groups, some, rows, cols), BF16), pltpu.VMEM((some, rows, tokens), BF16)
                ],
            ),
            out_shape=[flat_shape] * count,
            compiler_params=params,
            cost_estimate=cost(product * chunks, (2 + row_blocks) * chunks),
        )(place, *sum(grads, []), *sum(lefts, []))
        return [out[h::chunks] for h in range(chunks)]

    firsts = [p * blocks for p in range(chunks)]
    sent = [list(project(weight, first, blocks)) for weight in (right_w, left_w) for first in firsts]
    lefts = [exchange(pieces_of) for pieces_of in sent[chunks:]]
    halves, moved = [], []
    for part in range(chunks):
        got = tie(exchange(sent[part]), moved, *sent[part + 1:part + 1 + chunks])[0]
        before, beside = (moved + lefts[0][1:2], lefts[0][2:] + lefts[-1][2:3]) if part else ([], [])
        halves.append(all_rows(gather(got), before, beside))
        moved = halves[-1][cores:]
    right = [half[u] for u in range(row_blocks) for half in halves]
    sigms, grads, backs = [], [], []
    for first, left in zip(firsts, lefts):
        *grad_comb, sigm = middle(exchange(combine(left)), first)
        sigms.append(sigm)
        grads.append(exchange(grad_comb))
    left_grads = []
    for part in range(chunks):
        backs.append(list(left_back(grads[part])))
        left_grads.append(exchange(backs[part]))
        if part == 0 and chunks > 1:
            grads[-1] = tie(grads[-1], backs[0], left_grads[0][1:2])[0]
    right_grads = [
        exchange(split(own_rows(partials, back[1:3]))) for partials, back in zip(right_back(grads, lefts), left_grads)
    ]
    out = jnp.zeros((rows, cols, chans), BF16)
    for first, left_grad, right_grad, sigm in zip(firsts, left_grads, right_grads, sigms):
        out = last(left_grad, right_grad, sigm, first, out)
    return out


def solution(mesh):
    spread = P(("rep", "row", "sub"), "ch", None)
    return jax.shard_map(
        functools.partial(local, 2),
        mesh=mesh,
        in_specs=(spread, spread, P("rep"), P(), P(), P(), P(), P()),
        out_specs=spread,
        check_vma=False,
    )
```

```python
import functools

import jax
import jax.numpy as jnp
from jax import lax
from jax.experimental import pallas as pl
from jax.experimental.pallas import tpu as pltpu
from jax.sharding import PartitionSpec as P

epsilon = 1e-05
F32 = jnp.float32
BF16 = jnp.bfloat16
VMEM_LIMIT = 56 * 1024 * 1024
ROWS = ("row", "sub")


def dot(a, b, ca, cb):
    return lax.dot_general(a, b, (((ca,), (cb,)), ((), ())), preferred_element_type=F32)


def turn(block):
    return jnp.swapaxes(block.astype(F32), 0, 1)


def norm_rows(pair_block, gain):
    x = pair_block.astype(F32)
    center = x - jnp.mean(x, axis=1, keepdims=True)
    scaled = lax.rsqrt(jnp.mean(center * center, axis=1, keepdims=True) + epsilon)
    hat = center * scaled
    return hat, scaled, (hat * gain).astype(BF16)


def rows_of(ref, first, count):
    block = ref[first:first + count]
    return block.reshape(count * block.shape[1], block.shape[2])


def load_chan(refs, first, count):
    parts = [jnp.concatenate([ref[first + t].astype(F32) for ref in refs], axis=0) for t in range(count)]
    return parts[0] if count == 1 else jnp.concatenate(parts, axis=1)


def store_chan(refs, first, count, value):
    _, own, cols = refs[0].shape
    for s, ref in enumerate(refs):
        group = value[s * own:(s + 1) * own].astype(BF16)
        for t in range(count):
            ref[first + t] = group[:, t * cols:(t + 1) * cols] if count > 1 else group


def project_kernel(step, pair_ref, mask_ref, gain_ref, weight_ref, *out_refs):
    rows, cols, chans = pair_ref.shape
    for first in range(0, rows, step):
        _, _, normed = norm_rows(rows_of(pair_ref, first, step), gain_ref[...])
        both = dot(weight_ref[...], normed, 1, 1)
        mask = mask_ref[0, :, first * cols:(first + step) * cols]
        store_chan(out_refs, first, step, mask * jax.nn.sigmoid(both[chans:]) * both[:chans])


def middle_kernel(
    step, groups, pair_ref, gout_ref, gain_ref, gate_t_ref, out_w_ref, out_t_ref, out_gain_ref, eye_ref, *refs
):
    comb_refs, gcomb_refs, sigm_ref = refs[:groups], refs[groups:2 * groups], refs[2 * groups]
    rows, cols, chans = pair_ref.shape
    out_gain = out_gain_ref[...]
    for first in range(0, rows, step):
        _, _, normed = norm_rows(rows_of(pair_ref, first, step), gain_ref[...])
        gate = jax.nn.sigmoid(dot(gate_t_ref[...], normed, 1, 1))
        gout = dot(eye_ref[...], rows_of(gout_ref, first, step), 1, 1)
        comb = load_chan(comb_refs, first, step)
        center = comb - jnp.mean(comb, axis=0, keepdims=True)
        scaled = lax.rsqrt(jnp.mean(center * center, axis=0, keepdims=True) + epsilon)
        hat = center * scaled
        lin = dot(out_t_ref[...], (hat * out_gain).astype(BF16), 1, 0)
        grad_lin = (gout * gate).astype(BF16)
        h = dot(out_w_ref[...], grad_lin, 1, 0) * out_gain
        grad = scaled * (
            h - jnp.mean(h, axis=0, keepdims=True) - hat * jnp.mean(h * hat, axis=0, keepdims=True)
        )
        store_chan(gcomb_refs, first, step, grad)
        sigm = (gout * lin * gate * (1.0 - gate)).astype(BF16)
        for t in range(step):
            sigm_ref[first + t] = sigm[:, t * cols:(t + 1) * cols] if step > 1 else sigm


def last_kernel(step, groups, pair_ref, sigm_ref, mask_ref, gain_ref, weight_ref, held_ref, *refs):
    del held_ref
    left_refs, right_refs, out_ref = refs[:groups], refs[groups:2 * groups], refs[2 * groups]
    rows, cols, chans = pair_ref.shape
    gain = gain_ref[...]
    weight = weight_ref[...]
    for first in range(0, rows, step):
        hat, scaled, normed = norm_rows(rows_of(pair_ref, first, step), gain)
        mask = mask_ref[0, :, first * cols:(first + step) * cols]
        proj = dot(weight[:4 * chans], normed, 1, 1)
        terms = []
        for which, piece_refs in enumerate((left_refs, right_refs)):
            grad = load_chan(piece_refs, first, step) * mask
            value = proj[2 * which * chans:(2 * which + 1) * chans]
            gate = jax.nn.sigmoid(proj[(2 * which + 1) * chans:(2 * which + 2) * chans])
            through = grad * gate
            terms += [through.astype(BF16), (through * value * (1.0 - gate)).astype(BF16)]
        parts = [sigm_ref[first + t] for t in range(step)]
        terms.append(parts[0] if step == 1 else jnp.concatenate(parts, axis=1))
        g = dot(jnp.concatenate(terms, axis=0), weight, 0, 0) * gain
        grad_in = scaled * (
            g - jnp.mean(g, axis=1, keepdims=True) - hat * jnp.mean(g * hat, axis=1, keepdims=True)
        )
        out_ref[first:first + step] = grad_in.reshape(step, cols, chans).astype(BF16)


def gather_kernel(*refs):
    out_ref = refs[-1]
    cols = refs[0].shape[2]
    for s, ref in enumerate(refs[:-1]):
        out_ref[:, :, s * cols:(s + 1) * cols] = turn(ref[...]).astype(BF16)


def split_kernel(terms, *refs):
    in_refs, out_refs = refs[:terms], refs[terms:]
    cols = out_refs[0].shape[2]
    for s, ref in enumerate(out_refs):
        part = slice(s * cols, (s + 1) * cols)
        total = in_refs[0][:, :, part].astype(F32)
        for other in in_refs[1:]:
            total += other[:, :, part].astype(F32)
        ref[...] = turn(total.astype(BF16)).astype(BF16)


def block_of(right_refs, chunks, u, b, c, cols):
    parts = [ref[c] for ref in right_refs[u * chunks:(u + 1) * chunks]]
    rows = parts[0] if chunks == 1 else jnp.concatenate(parts, axis=0)
    return rows[b * cols:(b + 1) * cols]


def combine_kernel(groups, peers, chunks, place_ref, *refs):
    count = peers * chunks
    right_refs, left_refs, out_refs = refs[:count], refs[count:count + groups], refs[count + groups:-2]
    left_buf, sums = refs[-2:]
    rows, own, cols = left_refs[0].shape
    span = groups // peers
    for s, ref in enumerate(left_refs):
        left_buf[:, :, s * cols:(s + 1) * cols] = turn(ref[...]).astype(BF16)
    for n in range(groups):
        place = place_ref[n]
        for c in range(own):
            sums[place, c] = dot(left_buf[c], block_of(right_refs, chunks, n // span, n % span, c, cols), 1, 1)
    for s, ref in enumerate(out_refs):
        ref[...] = turn(sums[s]).astype(BF16)


def left_kernel(groups, peers, chunks, place_ref, *refs):
    count = peers * chunks
    right_refs, grad_refs, out_refs = refs[:count], refs[count:count + groups], refs[count + groups:-2]
    grads, sums = refs[-2:]
    rows, own, cols = grad_refs[0].shape
    span = groups // peers
    for s, ref in enumerate(grad_refs):
        grads[s] = turn(ref[...]).astype(BF16)
    for c in range(own):
        total = 0.0
        for n in range(groups):
            block = block_of(right_refs, chunks, n // span, n % span, c, cols)
            total += dot(grads[place_ref[n], c], block, 1, 0)
        sums[c] = total
    for s, ref in enumerate(out_refs):
        ref[...] = turn(sums[:, :, s * cols:(s + 1) * cols]).astype(BF16)


def right_kernel(groups, peers, chunks, place_ref, *refs):
    count = groups * chunks
    grad_refs, left_refs, out_refs = refs[:count], refs[count:2 * count], refs[2 * count:-2]
    grads, left_buf = refs[-2:]
    rows, own, cols = grad_refs[0].shape
    span = groups // peers
    for n, (grad_ref, left_ref) in enumerate(zip(grad_refs, left_refs)):
        piece, s = divmod(n, groups)
        part = slice(piece * rows, (piece + 1) * rows)
        grads[s, :, part] = turn(grad_ref[...]).astype(BF16)
        left_buf[:, part, s * cols:(s + 1) * cols] = turn(left_ref[...]).astype(BF16)
    for n in range(groups):
        place = place_ref[n]
        u, b = divmod(n, span)
        for c in range(own):
            total = dot(grads[place, c], left_buf[c], 0, 0).astype(BF16)
            for h in range(chunks):
                low, high = max(b * cols, h * rows), min((b + 1) * cols, (h + 1) * rows)
                if low < high:
                    out_refs[u * chunks + h][c, low - h * rows:high - h * rows] = total[
                        low - b * cols:high - b * cols
                    ]


def local(chunks, pair, grad_out, token_mask, ln_gain, proj_weights, gate_weight, out_weight, out_gain):
    rows, cols, chans = pair.shape
    groups = lax.axis_size("ch")
    sides, cores = lax.axis_size("row"), lax.axis_size("sub")
    row_blocks = sides * cores
    own = chans // groups
    tokens = rows * row_blocks
    part_rows = rows // chunks
    block = min(8, part_rows)
    blocks = part_rows // block
    step = 4 if cols % 128 == 0 and block % 4 == 0 else 1
    some = 16 if own % 16 == 0 else own
    z = lax.axis_index("ch")
    span = groups // row_blocks
    me = lax.axis_index(ROWS)
    place = jnp.stack([z ^ ((me ^ (n // span)) * span + n % span) for n in range(groups)]).astype(jnp.int32)

    def mine(array, axis):
        parts = [lax.dynamic_slice_in_dim(array, (z ^ s) * own, own, axis) for s in range(groups)]
        return jnp.concatenate(parts, axis=axis)

    mask_float = token_mask.astype(F32)
    row_mask = lax.dynamic_slice_in_dim(mask_float, lax.axis_index(ROWS) * rows, rows)
    col_mask = lax.dynamic_slice_in_dim(mask_float, z * cols, cols)
    mask = (row_mask[:, None] * col_mask[None, :]).reshape(rows // block, 1, block * cols)
    gain = ln_gain.reshape(1, chans)
    proj_t = mine(jnp.swapaxes(proj_weights, 1, 2), 1)
    left_w = proj_t[:2].reshape(2 * chans, chans)
    right_w = proj_t[2:].reshape(2 * chans, chans)
    gate_t = gate_weight.T
    all_w = jnp.concatenate([left_w, right_w, gate_t], axis=0)
    out_w = mine(out_weight, 0)
    out_t = out_w.T
    gain_col = mine(out_gain, 0).reshape(chans, 1)
    eye = jnp.eye(chans, dtype=BF16)

    params = pltpu.CompilerParams(vmem_limit_bytes=VMEM_LIMIT)

    def cost(flops, arrays):
        return pl.CostEstimate(
            flops=flops, bytes_accessed=arrays * part_rows * cols * chans * 2, transcendentals=0
        )

    pairs = part_rows * cols

    def row_spec(first):
        return pl.BlockSpec((block, cols, chans), lambda s: (first + s, 0, 0))

    def mask_spec(first):
        return pl.BlockSpec((1, 1, block * cols), lambda s: (first + s, 0, 0))

    def whole(array):
        return pl.BlockSpec(array.shape, lambda s: (0,) * array.ndim)

    piece_spec = pl.BlockSpec((block, own, cols), lambda s: (s, 0, 0))
    sigm_spec = pl.BlockSpec((block, chans, cols), lambda s: (s, 0, 0))

    def pieces(count):
        return [jax.ShapeDtypeStruct((count, own, cols), BF16)] * groups

    def project(weight, first, count):
        return pl.pallas_call(
            functools.partial(project_kernel, step),
            grid=(count,),
            in_specs=[row_spec(first), mask_spec(first), whole(gain), whole(weight)],
            out_specs=[piece_spec] * groups,
            out_shape=pieces(count * block),
            compiler_params=params,
            cost_estimate=cost(4 * chans * chans * count * block * cols, 2 * count // blocks),
        )(pair, mask, gain, weight)

    def middle(comb, first):
        return pl.pallas_call(
            functools.partial(middle_kernel, step, groups),
            grid=(blocks,),
            in_specs=[row_spec(first), row_spec(first), whole(gain), whole(gate_t), whole(out_w),
                      whole(out_t), whole(gain_col), whole(eye)] + [piece_spec] * groups,
            out_specs=[piece_spec] * groups + [sigm_spec],
            out_shape=pieces(part_rows) + [jax.ShapeDtypeStruct((part_rows, chans, cols), BF16)],
            compiler_params=params,
            cost_estimate=cost(8 * chans * chans * pairs, 5),
        )(pair, grad_out, gain, gate_t, out_w, out_t, gain_col, eye, *comb)

    def last(left_grad, right_grad, sigm, first, held):
        return pl.pallas_call(
            functools.partial(last_kernel, step, groups),
            grid=(blocks,),
            in_specs=[row_spec(first), sigm_spec, mask_spec(first), whole(gain), whole(all_w),
                      pl.BlockSpec(memory_space=pl.ANY)] + [piece_spec] * (2 * groups),
            out_specs=row_spec(first),
            out_shape=jax.ShapeDtypeStruct((rows, cols, chans), BF16),
            input_output_aliases={5: 0},
            compiler_params=params,
            cost_estimate=cost(18 * chans * chans * pairs, 5),
        )(pair, sigm, mask, gain, all_w, held, *left_grad, *right_grad)

    def exchange(sent):
        return [sent[0]] + [
            lax.ppermute(sent[s], "ch", [(a, a ^ s) for a in range(groups)]) for s in range(1, groups)
        ]

    def chan_spec(count):
        return pl.BlockSpec((count, some, cols), lambda g, *_: (0, g, 0))

    flat_spec = pl.BlockSpec((some, part_rows, tokens), lambda g, *_: (g, 0, 0))
    flat_shape = jax.ShapeDtypeStruct((own, part_rows, tokens), BF16)

    def gather(got):
        return pl.pallas_call(
            gather_kernel,
            grid=(own // some,),
            in_specs=[chan_spec(part_rows)] * groups,
            out_specs=flat_spec,
            out_shape=flat_shape,
            compiler_params=params,
            cost_estimate=cost(0, 2),
        )(*got)

    def split(terms):
        return pl.pallas_call(
            functools.partial(split_kernel, len(terms)),
            grid=(own // some,),
            in_specs=[flat_spec] * len(terms),
            out_specs=[chan_spec(part_rows)] * groups,
            out_shape=pieces(part_rows),
            compiler_params=params,
            cost_estimate=cost(0, 1 + len(terms)),
        )(*terms)

    def tie(*lists):
        values = iter(lax.optimization_barrier(tuple(sum(lists, []))))
        return [[next(values) for _ in part] for part in lists]

    def swap(array, axis, by):
        return lax.ppermute(array, axis, [(a, a ^ by) for a in range(lax.axis_size(axis))])

    def all_rows(array, before, beside):
        blocks = [swap(array, "sub", c) if c else array for c in range(cores)]
        sent = tie([array], blocks[1:], before)[0][0]
        for x in range(1, sides):
            came = tie([swap(sent, "row", x)], beside)[0][0]
            blocks += [swap(came, "sub", c) if c else came for c in range(cores)]
        return blocks

    def own_rows(partials, before):
        terms = []
        for x in range(sides):
            of_cores = [swap(partials[x * cores + c], "sub", c) if c else partials[x * cores] for c in range(cores)]
            if x:
                total = sum(term.astype(F32) for term in of_cores).astype(BF16)
                terms.append(swap(tie([total], before)[0][0], "row", x))
            else:
                terms += of_cores
        return terms

    product = 2 * part_rows * tokens * tokens * own

    def with_right(kernel, got, scratch):
        return pl.pallas_call(
            functools.partial(kernel, groups, row_blocks, chunks),
            grid_spec=pltpu.PrefetchScalarGridSpec(
                num_scalar_prefetch=1, grid=(own // some,),
                in_specs=[flat_spec] * (row_blocks * chunks) + [chan_spec(part_rows)] * groups,
                out_specs=[chan_spec(part_rows)] * groups,
                scratch_shapes=scratch,
            ),
            out_shape=pieces(part_rows),
            compiler_params=params,
            cost_estimate=cost(product, 2 + row_blocks * chunks),
        )(place, *right, *got)

    def combine(left):
        return with_right(combine_kernel, left, [
            pltpu.VMEM((some, part_rows, tokens), BF16), pltpu.VMEM((groups, some, part_rows, cols), F32)
        ])

    def left_back(grad):
        return with_right(left_kernel, grad, [
            pltpu.VMEM((groups, some, part_rows, cols), BF16), pltpu.VMEM((some, part_rows, tokens), F32)
        ])

    def right_back(grads, lefts):
        count = row_blocks * chunks
        out = pl.pallas_call(
            functools.partial(right_kernel, groups, row_blocks, chunks),
            grid_spec=pltpu.PrefetchScalarGridSpec(
                num_scalar_prefetch=1, grid=(own // some,),
                in_specs=[chan_spec(part_rows)] * (2 * groups * chunks),
                out_specs=[flat_spec] * count,
                scratch_shapes=[
                    pltpu.VMEM((groups, some, rows, cols), BF16), pltpu.VMEM((some, rows, tokens), BF16)
                ],
            ),
            out_shape=[flat_shape] * count,
            compiler_params=params,
            cost_estimate=cost(product * chunks, (2 + row_blocks) * chunks),
        )(place, *sum(grads, []), *sum(lefts, []))
        return [out[h::chunks] for h in range(chunks)]

    firsts = [p * blocks for p in range(chunks)]
    sent = [list(project(weight, first, blocks)) for weight in (right_w, left_w) for first in firsts]
    lefts = [exchange(pieces_of) for pieces_of in sent[chunks:]]
    halves, moved = [], []
    rights = [exchange(pieces_of) for pieces_of in sent[:chunks]]
    for part in range(chunks):
        got = tie(rights[part], moved, *sent[part + 1:part + 1 + chunks])[0]
        before, beside = (moved + lefts[0][1:2], lefts[0][2:] + lefts[-1][2:3]) if part else ([], rights[-1][1:])
        halves.append(all_rows(gather(got), before, beside))
        moved = halves[-1][cores::cores]
    right = [half[u] for u in range(row_blocks) for half in halves]
    sigms, grads, backs = [], [], []
    for first, left in zip(firsts, lefts):
        *grad_comb, sigm = middle(exchange(combine(left)), first)
        sigms.append(sigm)
        grads.append(exchange(grad_comb))
    left_grads = []
    for part in range(chunks):
        backs.append(list(left_back(grads[part])))
        left_grads.append(exchange(backs[part]))
        if part == 0 and chunks > 1:
            grads[-1] = tie(grads[-1], backs[0], left_grads[0][1:2])[0]
    right_grads = [
        exchange(split(own_rows(partials, back[1:3]))) for partials, back in zip(right_back(grads, lefts), left_grads)
    ]
    out = jnp.zeros((rows, cols, chans), BF16)
    for first, left_grad, right_grad, sigm in zip(firsts, left_grads, right_grads, sigms):
        out = last(left_grad, right_grad, sigm, first, out)
    return out


def solution(mesh):
    spread = P(("rep", "row", "sub"), "ch", None)
    return jax.shard_map(
        functools.partial(local, 2),
        mesh=mesh,
        in_specs=(spread, spread, P("rep"), P(), P(), P(), P(), P()),
        out_specs=spread,
        check_vma=False,
    )
```
